256 devices in a mesh: dp: 16 (over y, x), vocab: 16 (over z, core).
Axes of the slice: x: 4, y: 4, z: 8, core: 2. Of those that a mesh axis runs over, the one named last changes fastest.
Arguments:
- hidden: bfloat16 [4096, 3072], P('dp', 'vocab'), may hold values from -64 to 64
- input_grad: bfloat16 [4096, 3072], P('dp', 'vocab'), may hold values from -6 to 6
- embedding: bfloat16 [128256, 3072], P(('dp', 'vocab')), may hold values from -1 to 1
- vocab_proj: bfloat16 [128256, 64], P(('dp', 'vocab')), may hold values from -0.359375 to 0.359375
- feature_proj: bfloat16 [3072, 64], P('vocab'), may hold values from -0.109375 to 0.109375
- token_ids: int32 [4096], P('dp'), may hold values from 0 to 128255
- targets: int32 [4096], P('dp'), may hold values from 0 to 128255
- doc_ids: int32 [4096], P('dp'), may hold values from 0 to 63, as said below
Outputs:
- doc_grads: float32 [64, 4096], P('dp')
The draws below stay inside these ranges and needn't reach their ends.
Inputs may be any that keep to these rules, and one draw needn't show every extreme that they name: `doc_ids`: never falls; the tokens of group g, positions g * 256 to (g + 1) * 256 - 1, belong to documents g * 4 to (g + 1) * 4 - 1, and each of these documents has one token or more.
All inputs are finite; a program needn't handle non-finite values.
Results may differ from the reference program's by a relative error of at most 0.0003.
Values may be sent and summed in bfloat16 or wider, within the bound.
A program may use at most 128 MiB of HBM per device.

```python
import math
import jax
import jax.numpy as jnp
import numpy as np
from jax import lax

V = 128256
D = 3072
KV = 64
KD = 64
TOK_DP = 256
DOC_DP = 4
TOKENS = 4096
DOCS = 64


def row_scales(source_key):
    scale_key = jax.random.fold_in(source_key, 101)
    spread = jnp.exp(jax.random.uniform(scale_key, (V,), jnp.float32, math.log(0.5), math.log(2.0)))
    return spread * (1.0 + 2.0 * jnp.arange(V, dtype=jnp.float32) / V)


def row_noise(source_key, row_list):
    noise_key = jax.random.fold_in(source_key, 55)

    def one_row(number):
        return jax.random.normal(jax.random.fold_in(noise_key, number), (D,), jnp.float32)
    return jax.vmap(one_row)(row_list)


def draw_hidden(key, part):
    key = jax.random.fold_in(key, 7)
    token_scale = jnp.exp(jax.random.uniform(jax.random.fold_in(key, 1), (TOKENS,), jnp.float32, math.log(0.3), math.log(3.0)))
    values = jax.random.normal(jax.random.fold_in(key, 2), (TOKENS, D), jnp.float32) * token_scale[:, None]
    return jnp.clip(values, -64.0, 64.0).astype(jnp.bfloat16)


def draw_embedding(key, part):
    source_key = key
    scales = row_scales(source_key)
    row_list = jnp.arange(V)
    noise = row_noise(source_key, row_list)
    return jnp.clip(noise * (scales / math.sqrt(D))[:, None], -1.0, 1.0).astype(jnp.bfloat16)


def draw_doc_ids(key, part):
    key = jax.random.fold_in(key, 23)
    group_count = TOKENS // TOK_DP

    def one_group(group_key, group_index):
        shuffled = jax.random.permutation(group_key, TOK_DP - 1) + 1
        cuts = shuffled[:DOC_DP - 1]
        position = jnp.arange(TOK_DP)
        local_ids = jnp.sum((position[:, None] >= cuts[None, :]).astype(jnp.int32), axis=1)
        return local_ids + group_index * DOC_DP
    group_keys = jax.random.split(key, group_count)
    return jax.vmap(one_group)(group_keys, jnp.arange(group_count)).reshape(-1).astype(jnp.int32)


def set_ends(entries, key, low, largest):
    dims = entries.shape
    place = [jax.random.randint(jax.random.fold_in(key, axis), (), 0, dims[axis]) for axis in range(len(dims))]
    entries = entries.at[tuple(place)].set(low)
    longest = dims.index(max(dims))
    place[longest] = (place[longest] + 1) % dims[longest]
    return entries.at[tuple(place)].set(largest)


def levels(rng, shape, cuts, smallest, largest):
    level, own = 1.0, jax.random.fold_in(rng, 6)
    for dim, blocks in cuts:
        heights = jnp.exp(jax.random.uniform(jax.random.fold_in(own, dim), (blocks,), jnp.float32, smallest / len(cuts), largest / len(cuts)))
        level = level * jnp.repeat(heights, shape[dim] // blocks).reshape([-1 if axis == dim else 1 for axis in range(len(shape))])
    return level


def wide_ids(stream_key, extent, amount, slope):
    loads = [min(1 << octave, amount + 1 - (1 << octave)) * (1 << 20) // math.isqrt((1 << octave) ** slope) + 1 for octave in range((amount + 1).bit_length()) if 1 << octave <= amount]
    deviation = 1 + sum(loads) // (1 << 30)
    grid = np.cumsum(np.array([max(1, weight // deviation) for weight in loads]))
    pick = jax.random.randint(jax.random.fold_in(stream_key, 1), extent, 0, int(grid[len(loads) - 1]))
    start = jnp.left_shift(1, jnp.searchsorted(jnp.asarray(grid, jnp.int32), pick, side="right").astype(jnp.int32))
    rank = start - 1 + jax.random.randint(jax.random.fold_in(stream_key, 4), extent, 0, 1 << 30) % jnp.minimum(start, amount + 1 - start)
    return jax.random.permutation(jax.random.fold_in(stream_key, 2), amount)[rank].astype(jnp.int32)


def bell_draw(rng, dims, scale, reach, cuts=(), held_as=jnp.bfloat16):
    entries = scale * jax.random.normal(rng, dims, jnp.float32)
    if cuts:
        entries = entries * levels(rng, dims, cuts, -0.22, 0.18)
    return jnp.clip(entries, -reach, reach).astype(held_as)


def setup_inputs(seed: int = 0) -> dict:
    key_list = jax.random.split(jax.random.key(seed), 9)
    hidden = draw_hidden(jax.random.fold_in(key_list[8], 71), 0)
    input_grad = bell_draw(key_list[1], (TOKENS, D), 1.0, 6.0, ((0, 16), (1, 16)))
    embedding = draw_embedding(jax.random.fold_in(key_list[8], 71), 0)
    vocab_proj = bell_draw(key_list[3], (V, KV), 0.06, 0.359375, ((0, 256),))
    feature_proj = bell_draw(key_list[4], (D, KD), D ** -0.5, 0.109375, ((0, 16),))
    token_ids = set_ends(wide_ids(key_list[5], (TOKENS,), V, 2), jax.random.fold_in(key_list[5], 3), 0, V - 1).astype(jnp.int32)
    targets = set_ends(wide_ids(key_list[6], (TOKENS,), V, 2), jax.random.fold_in(key_list[6], 3), 0, V - 1).astype(jnp.int32)
    doc_ids = draw_doc_ids(jax.random.fold_in(key_list[8], 71), 0)
    return dict(hidden=hidden, input_grad=input_grad, embedding=embedding, vocab_proj=vocab_proj, feature_proj=feature_proj, token_ids=token_ids, targets=targets, doc_ids=doc_ids)


PRECISE = lax.Precision.HIGHEST


def contract_rows(left_mat, right_mat):
    return lax.dot_general(left_mat, right_mat, (((1,), (1,)), ((), ())), preferred_element_type=jnp.float32)


def reference(hidden, input_grad, embedding, vocab_proj, feature_proj, token_ids, targets, doc_ids):
    stride = V // 16

    def sweep(running, counter):
        maximum, summed_exp, weighted = running
        anchor = counter * stride
        block_rows = lax.dynamic_slice_in_dim(embedding, anchor, stride, 0)
        proj_table = lax.dynamic_slice_in_dim(vocab_proj, anchor, stride, 0).astype(jnp.float32)
        logits = contract_rows(hidden, block_rows)
        highest = jnp.maximum(maximum, jnp.max(logits, axis=1))
        shrink = jnp.exp(maximum - highest)
        scaled = jnp.exp(logits - highest[:, None])
        weighted = weighted * shrink[:, None] + jnp.dot(scaled, proj_table, precision=PRECISE, preferred_element_type=jnp.float32)
        return (highest, summed_exp * shrink + jnp.sum(scaled, axis=1), weighted), None

    initial = (jnp.full((TOKENS,), -jnp.inf, jnp.float32), jnp.zeros((TOKENS,), jnp.float32), jnp.zeros((TOKENS, KV), jnp.float32))
    (maximum, summed_exp, weighted), _ = lax.scan(sweep, initial, jnp.arange(16, dtype=jnp.int32))
    head_side = weighted / summed_exp[:, None] - vocab_proj[targets].astype(jnp.float32)
    embed_side = vocab_proj[token_ids].astype(jnp.float32)
    hidden_side = jnp.dot(hidden, feature_proj, preferred_element_type=jnp.float32)
    grad_side = jnp.dot(input_grad, feature_proj, preferred_element_type=jnp.float32)
    membership = (doc_ids[:, None] == jnp.arange(DOCS, dtype=jnp.int32)[None, :]).astype(jnp.float32)
    head_part = jnp.einsum("tdi,tj->dij", membership[:, :, None] * head_side[:, None, :], hidden_side, precision=PRECISE)
    embed_part = jnp.einsum("tdi,tj->dij", membership[:, :, None] * embed_side[:, None, :], grad_side, precision=PRECISE)
    return (head_part + embed_part).reshape(DOCS, KV * KD)
```

```python
import jax
import jax.numpy as jnp
from jax import lax
from jax.experimental import pallas as pl
from jax.experimental.pallas import tpu as pltpu
from jax.sharding import PartitionSpec as P

MESH = pl.DeviceIdType.MESH
PRECISE = lax.Precision.HIGHEST
V_ROWS = 501
PAD_ROWS = 512
D = 3072
SLICE = 384
NEAR = ((1, 1), (2, 2), (3, 3))


def logits_of(tokens, rows):
    return lax.dot_general(
        tokens, rows, (((1,), (1,)), ((), ())), preferred_element_type=jnp.float32
    )


def mix(parts):
    peaks = [part[:, 65:66] for part in parts]
    top = peaks[0]
    for peak in peaks[1:]:
        top = jnp.maximum(top, peak)
    total = parts[0] * jnp.exp(peaks[0] - top)
    for part, peak in zip(parts[1:], peaks[1:]):
        total = total + part * jnp.exp(peak - top)
    lane = lax.broadcasted_iota(jnp.int32, total.shape, 1)
    return jnp.where(lane == 65, top, total)


def kernel(
    hid_ref, grad_ref, fp_ref, pe_ref, tgt_ref, ids_ref, docs_ref, emb_ref, out_ref,
    rx, gath, hall, emb, pe, pet, idb, part, look, look_in, part_in, q1, q1_in, q2, q2_in, tok, feat, side, side_in, sd_in, sz, sz_in,
    sem_l, sem_c, sem_z, sem_1, sem_2, sem_i, sem_s, sem_r, sem_q, sem_t,
):
    g, v = lax.axis_index("dp"), lax.axis_index("vocab")
    x, y = lax.rem(g, 4), lax.div(g, 4)
    z, c = lax.div(v, 2), lax.rem(v, 2)

    def dev(dx=0, dy=0, dz=0, dc=0):
        return (
            lax.rem(y + dy, 4) * 4 + lax.rem(x + dx, 4),
            lax.rem(z + dz, 8) * 2 + lax.rem(c + dc, 2),
        )

    def remote(src, dst, send, recv, to):
        return pltpu.make_async_remote_copy(
            src_ref=src, dst_ref=dst, send_sem=send, recv_sem=recv, device_id=to, device_id_type=MESH
        )

    started = []

    def go(copy):
        copy.start()
        started.append(copy)
        return copy

    emb_local = pltpu.make_async_copy(emb_ref, emb.at[c], sem_l.at[0])
    emb_local.start()
    pe[c] = pe_ref[...]
    first = c == 0
    row_id = lax.broadcasted_iota(jnp.int32, (8, 128), 0)
    own_tgt = jnp.where(first, tgt_ref[0:1], tgt_ref[1:2])
    own_ids = jnp.where(first, ids_ref[0:1], ids_ref[1:2])
    idb[y, x] = jnp.where(row_id == 0, own_tgt, own_ids)

    barrier = pltpu.get_barrier_semaphore()
    peers = [dev(dc=1)] + [dev(dz=k) for k in range(1, 8)]
    peers += [dev(dx=k) for k in range(1, 4)] + [dev(dy=k) for k in range(1, 4)]
    for peer in peers:
        pl.semaphore_signal(barrier, inc=1, device_id=peer, device_id_type=MESH)
    pl.semaphore_wait(barrier, len(peers))

    other = pl.multiple_of((1 - c) * 128, 128)
    mine = pl.multiple_of(c * 128, 128)
    swap = go(remote(hid_ref.at[pl.ds(other, 128)], rx, sem_c.at[0], sem_c.at[1], dev(dc=1)))
    ids_1 = [
        go(remote(idb.at[y, x], idb.at[y, x], sem_i.at[0, 0, k - 1], sem_i.at[0, 1, k - 1], dev(dx=k)))
        for k in range(1, 4)
    ]
    pe_swap = go(remote(pe.at[c], pe.at[c], sem_c.at[2], sem_c.at[3], dev(dc=1)))
    swap.wait_recv()
    own_half, got_half = hid_ref[pl.ds(mine, 128), :], rx[...]
    left = jnp.where(first, own_half, got_half)
    right = jnp.where(first, got_half, own_half)

    def columns(zz):
        return pl.ds(pl.multiple_of(lax.rem(zz, 8) * SLICE, 128), SLICE)

    gath[:, columns(z)] = jnp.concatenate([left, right], axis=1)

    def ring(direction, step):
        if direction == 0:
            where, to = columns(z + 8 - (step - 1)), dev(dz=1)
        else:
            where, to = columns(z + step - 1), dev(dz=7)
        block = gath.at[:, where]
        return remote(block, block, sem_z.at[direction, 0, step - 1], sem_z.at[direction, 1, step - 1], to)

    rings = {}
    for direction in (0, 1):
        rings[direction, 1] = go(ring(direction, 1))
    emb_swap = go(remote(emb_ref, emb.at[c], sem_c.at[4], sem_c.at[5], dev(dc=1)))

    side[:, :64] = jnp.dot(hid_ref[...], fp_ref[...], preferred_element_type=jnp.float32)
    side[:, 64:] = jnp.dot(grad_ref[...], fp_ref[...], preferred_element_type=jnp.float32)
    side_swap = go(remote(side.at[pl.ds(other, 128)], sd_in, sem_c.at[6], sem_c.at[7], dev(dc=1)))

    for step in range(1, 4):
        for direction in (0, 1):
            rings[direction, step].wait_recv()
            if step < 3 or direction == 0:
                rings[direction, step + 1] = go(ring(direction, step + 1))
        if step == 1:
            for copy in ids_1:
                copy.wait_recv()
            ids_2 = [
                go(remote(idb.at[y], idb.at[y], sem_i.at[1, 0, k - 1], sem_i.at[1, 1, k - 1], dev(dy=k)))
                for k in range(1, 4)
            ]
        if step == 2:
            side_swap.wait_recv()
            both = side[pl.ds(mine, 128), :] + sd_in[...]
            for zz in range(8):
                for half in range(2):
                    sz[zz, half] = both[half * 64 + zz * 8 : half * 64 + zz * 8 + 8]
            side_z = [
                go(remote(sz.at[lax.rem(z + k, 8)], sz_in.at[k], sem_s.at[0, 0, k - 1], sem_s.at[0, 1, k - 1], dev(dz=k)))
                for k in range(1, 8)
            ]
    rings[0, 4].wait_recv()

    out_at, in_at = (y, x), (x, y)

    def inner(half, k):
        return dev(dx=k) if half == 0 else dev(dy=k)

    def outer(half, k):
        return dev(dy=k) if half == 0 else dev(dx=k)

    STEP = (1, 3)

    def first_own(half, way):
        return remote(
            gath.at[pl.ds(half * 64, 64)], hall.at[half, out_at[half], in_at[half]],
            sem_1.at[half, way, 0, 0], sem_1.at[half, way, 1, 0], inner(half, STEP[way]),
        )

    def first_on(half, way):
        from_pos = lax.rem(in_at[half] + 4 - STEP[way], 4)
        block = hall.at[half, out_at[half], from_pos, pl.ds(way * 32, 32)]
        return remote(block, block, sem_1.at[half, way, 0, 1], sem_1.at[half, way, 1, 1], inner(half, STEP[way]))

    def second_own(half, way, k):
        pos = lax.rem(in_at[half] + k, 4)
        dst = hall.at[half, out_at[half], pos]
        src = gath.at[pl.ds(half * 64, 64)] if k == 0 else dst
        return remote(src, dst, sem_2.at[half, way, 0, 0, k], sem_2.at[half, way, 1, 0, k], outer(half, STEP[way]))

    def second_on(half, way, k):
        pos = lax.rem(in_at[half] + k, 4)
        from_row = lax.rem(out_at[half] + 4 - STEP[way], 4)
        block = hall.at[half, from_row, pos, pl.ds(way * 32, 32)]
        return remote(
            block, block, sem_2.at[half, way, 0, 1, k], sem_2.at[half, way, 1, 1, k], outer(half, STEP[way])
        )

    HALVES, WAYS = (0, 1), (0, 1)
    near = {(h, w): go(first_own(h, w)) for h in HALVES for w in WAYS}
    for h in HALVES:
        for w in WAYS:
            go(second_own(h, w, 0))
    keep = [
        pltpu.make_async_copy(gath.at[pl.ds(h * 64, 64)], hall.at[h, out_at[h], in_at[h]], sem_l.at[1 + h])
        for h in HALVES
    ]
    for copy in keep:
        copy.start()

    pe_swap.wait_recv()
    for b in range(2):
        pet[b] = jnp.transpose(pe[b].astype(jnp.float32)).astype(jnp.bfloat16)

    far = {}
    for h in HALVES:
        for w in WAYS:
            near[h, w].wait_recv()
            far[h, w] = go(first_on(h, w))
    for k in (1, 3):
        for h in HALVES:
            for w in WAYS:
                go(second_own(h, w, k))

    sz_in[0] = sz[z]
    for copy in side_z:
        copy.wait_recv()
    total = sz_in[0]
    for k in range(1, 8):
        total = total + sz_in[k]
    feat[c, :, z] = total
    feat_z = [
        go(remote(feat.at[c, :, z], feat.at[c, :, z], sem_s.at[1, 0, k - 1], sem_s.at[1, 1, k - 1], dev(dz=k)))
        for k in range(1, 8)
    ]

    for h in HALVES:
        for w in WAYS:
            far[h, w].wait_recv()
    for h in HALVES:
        for w in WAYS:
            go(second_own(h, w, 2))
    for copy in feat_z:
        copy.wait_recv()
    feat_swap = go(remote(feat.at[c], feat.at[c], sem_c.at[8], sem_c.at[9], dev(dc=1)))

    for copy in ids_2:
        copy.wait_recv()
    row_base = (g * 16 + z * 2) * V_ROWS

    def look_up(group, carry):
        gy, gx = lax.div(group, 4), lax.rem(group, 4)
        ids = idb[gy, gx]
        wanted = jnp.concatenate([ids[0:1], ids[1:2]], axis=1) - row_base
        found = None
        for b in range(2):
            numbers = lax.broadcasted_iota(jnp.int32, (PAD_ROWS, 256), 0) + b * V_ROWS
            hit = jnp.where(numbers == wanted, 1.0, 0.0).astype(jnp.bfloat16)
            term = jnp.dot(pet[b, :64], hit, preferred_element_type=jnp.float32)
            found = term if found is None else found + term
        stacked = jnp.concatenate([found[:, :128], found[:, 128:]], axis=0)
        rows = jnp.transpose(stacked).astype(jnp.bfloat16)
        look[0, gy, gx] = rows[:64]
        look[1, gx, gy] = rows[64:]
        return carry

    lax.fori_loop(0, 16, look_up, 0)

    def look_send(half, k):
        return remote(
            look.at[half, lax.rem(out_at[half] + k, 4)], look_in.at[half, k - 1],
            sem_r.at[0, half, 0, k - 1], sem_r.at[0, half, 1, k - 1], outer(half, k),
        )

    look_sends = [go(look_send(h, k)) for h in HALVES for k in (1, 2, 3)]

    for copy in keep:
        copy.wait()
    emb_local.wait()
    emb_swap.wait_recv()

    def part_send(t, half, k, to):
        return remote(
            part.at[t], part_in.at[half, k - 1], sem_r.at[1, half, 0, k - 1], sem_r.at[1, half, 1, k - 1], to
        )

    def tile(t, carry):
        half, turn = lax.rem(t, 2), lax.div(t, 2)
        k = turn + lax.div(turn, 2) - 2 * lax.div(turn, 3)

        @pl.when(t == 2)
        def _():
            for kk in (0, 1, 3, 2):
                for h in HALVES:
                    for w in WAYS:
                        second_own(h, w, kk).wait_recv()
                        second_on(h, w, kk).start()

        @pl.when(t == 6)
        def _():
            for kk in (0, 1, 3, 2):
                for w in WAYS:
                    second_on(0, w, kk).wait_recv()

        @pl.when(t == 7)
        def _():
            for kk in (0, 1, 3, 2):
                for w in WAYS:
                    second_on(1, w, kk).wait_recv()

        row = lax.rem(y * (1 - half) + x * half + k, 4)
        tokens = hall[half, row].reshape(256, D)
        l0 = logits_of(tokens, emb[0])
        l1 = logits_of(tokens, emb[1])
        top = jnp.maximum(jnp.max(l0, axis=1, keepdims=True), jnp.max(l1, axis=1, keepdims=True))
        acc = None
        for b, logits in enumerate((l0, l1)):
            scaled = jnp.exp(logits - top)
            coarse = scaled.astype(jnp.bfloat16)
            fine = (scaled - coarse.astype(jnp.float32)).astype(jnp.bfloat16)
            table = pe[b, :V_ROWS]
            for piece in (coarse, fine):
                term = jnp.dot(piece, table, preferred_element_type=jnp.float32)
                acc = term if acc is None else acc + term
        lane = lax.broadcasted_iota(jnp.int32, acc.shape, 1)
        part[t] = jnp.where(lane == 65, top, acc)

        @pl.when(turn > 0)
        def _():
            part_send(t, half, k, dev(dx=half * k, dy=(1 - half) * k)).start()

        return carry

    lax.fori_loop(0, 8, tile, 0)

    for copy in look_sends:
        copy.wait_recv()
    for h in HALVES:
        for k in (1, 2, 3):
            part_send(0, h, k, outer(h, k)).wait_recv()
        mixed = mix([part[h]] + [part_in[h, k] for k in range(3)])
        looked = look[h, out_at[h]].astype(jnp.float32)
        for k in range(3):
            looked = looked + look_in[h, k].astype(jnp.float32)
        q1[h, :, :, :128] = mixed.reshape(4, 64, 128)
        q1[h, :, :, 128:] = looked
        for k in (1, 2, 3):
            go(
                remote(
                    q1.at[h, lax.rem(in_at[h] + k, 4)], q1_in.at[h, k - 1],
                    sem_q.at[h, 0, k - 1], sem_q.at[h, 1, k - 1], inner(h, k),
                )
            )
    for h in HALVES:
        for k in (1, 2, 3):
            remote(q1.at[h, 0], q1_in.at[h, k - 1], sem_q.at[h, 0, k - 1], sem_q.at[h, 1, k - 1], inner(h, k)).wait_recv()
        own = q1[h, in_at[h]]
        mixed = mix([own[:, :128]] + [q1_in[h, k, :, :128] for k in range(3)])
        looked = own[:, 128:]
        for k in range(3):
            looked = looked + q1_in[h, k, :, 128:]
        q2[:, h, :, :128] = mixed.reshape(8, 8, 128)
        q2[:, h, :, 128:] = looked.reshape(8, 8, 128)
    q2_z = [
        go(remote(q2.at[lax.rem(z + k, 8)], q2_in.at[k - 1], sem_t.at[0, 0, k - 1], sem_t.at[0, 1, k - 1], dev(dz=k)))
        for k in range(1, 8)
    ]
    for copy in q2_z:
        copy.wait_recv()
    sums = [q2[z].reshape(16, 256)] + [q2_in[k].reshape(16, 256) for k in range(7)]
    mixed = mix([one[:, :128] for one in sums])
    looked = sums[0][:, 128:]
    for one in sums[1:]:
        looked = looked + one[:, 128:]
    head = mixed[:, :64] / mixed[:, 64:65] - looked[:, :64]
    tok[c, :, z] = jnp.concatenate([head, looked[:, 64:]], axis=1).reshape(2, 8, 128)
    tok_z = [
        go(remote(tok.at[c, :, z], tok.at[c, :, z], sem_t.at[1, 0, k - 1], sem_t.at[1, 1, k - 1], dev(dz=k)))
        for k in range(1, 8)
    ]
    for copy in tok_z:
        copy.wait_recv()
    tok_swap = go(remote(tok.at[c], tok.at[c], sem_c.at[10], sem_c.at[11], dev(dc=1)))
    feat_swap.wait_recv()
    tok_swap.wait_recv()

    turned = jnp.transpose(tok[...].reshape(256, 128))
    local = jnp.concatenate([docs_ref[0:1], docs_ref[1:2]], axis=1) - g * 4
    feats = feat[...].reshape(256, 128)
    member = [jnp.where(local == d, 1.0, 0.0) for d in range(4)]
    head_lhs = jnp.concatenate([turned[:64] * m for m in member], axis=0)
    embed_lhs = jnp.concatenate([turned[64:] * m for m in member], axis=0)
    out_ref[...] = jnp.dot(
        head_lhs, feats[:, :64], precision=PRECISE, preferred_element_type=jnp.float32
    ) + jnp.dot(embed_lhs, feats[:, 64:], precision=PRECISE, preferred_element_type=jnp.float32)

    for copy in started:
        copy.wait_send()
    for h in HALVES:
        for w in WAYS:
            for k in range(4):
                second_on(h, w, k).wait_send()
        for k in (1, 2, 3):
            part_send(0, h, k, outer(h, k)).wait_send()


def per_device(hidden, input_grad, embedding, vocab_proj, feature_proj, token_ids, targets, doc_ids):
    table = jnp.concatenate(
        [vocab_proj, jnp.ones((V_ROWS, 1), jnp.bfloat16), jnp.zeros((V_ROWS, 63), jnp.bfloat16)], axis=1
    )
    table = jnp.pad(table, ((0, PAD_ROWS - V_ROWS), (0, 0)))
    vmem = pl.BlockSpec(memory_space=pltpu.VMEM)
    bf16, f32, i32 = jnp.bfloat16, jnp.float32, jnp.int32
    dma = pltpu.SemaphoreType.DMA
    out = pl.pallas_call(
        kernel,
        out_shape=jax.ShapeDtypeStruct((256, 64), f32),
        in_specs=[vmem] * 7 + [pl.BlockSpec(memory_space=pl.ANY)],
        out_specs=vmem,
        scratch_shapes=[
            pltpu.VMEM((128, 192), bf16),
            pltpu.VMEM((128, D), bf16),
            pltpu.VMEM((2, 4, 4, 64, D), bf16),
            pltpu.VMEM((2, V_ROWS, D), bf16),
            pltpu.VMEM((2, PAD_ROWS, 128), bf16),
            pltpu.VMEM((2, 128, PAD_ROWS), bf16),
            pltpu.VMEM((4, 4, 8, 128), i32),
            pltpu.VMEM((8, 256, 128), f32),
            pltpu.VMEM((2, 4, 4, 64, 128), bf16),
            pltpu.VMEM((2, 3, 4, 64, 128), bf16),
            pltpu.VMEM((2, 3, 256, 128), f32),
            pltpu.VMEM((2, 4, 64, 256), f32),
            pltpu.VMEM((2, 3, 64, 256), f32),
            pltpu.VMEM((8, 2, 8, 256), f32),
            pltpu.VMEM((7, 2, 8, 256), f32),
            pltpu.VMEM((2, 2, 8, 8, 128), f32),
            pltpu.VMEM((2, 2, 8, 8, 128), f32),
            pltpu.VMEM((256, 128), f32),
            pltpu.VMEM((8, 2, 8, 128), f32),
            pltpu.VMEM((128, 128), f32),
            pltpu.VMEM((8, 2, 8, 128), f32),
            pltpu.VMEM((8, 2, 8, 128), f32),
            dma((3,)),
            dma((12,)),
            dma((2, 2, 4)),
            dma((2, 2, 2, 2)),
            dma((2, 2, 2, 2, 4)),
            dma((2, 2, 3)),
            dma((2, 2, 7)),
            dma((2, 2, 2, 3)),
            dma((2, 2, 3)),
            dma((2, 2, 7)),
        ],
        compiler_params=pltpu.CompilerParams(
            collective_id=0, has_side_effects=True, vmem_limit_bytes=60 * 2**20
        ),
        name="doc_grads",
    )(
        hidden, input_grad, feature_proj, table,
        targets.reshape(2, 128), token_ids.reshape(2, 128), doc_ids.reshape(2, 128), embedding,
    )
    return out.reshape(4, 4096)


def solution(mesh):
    placed = (
        P("dp", "vocab"),
        P("dp", "vocab"),
        P(("dp", "vocab"), None),
        P(("dp", "vocab"), None),
        P("vocab", None),
        P("dp"),
        P("dp"),
        P("dp"),
    )
    return jax.shard_map(
        per_device, mesh=mesh, in_specs=placed, out_specs=P("dp", None), check_vma=False
    )
```

```python
import jax
import jax.numpy as jnp
from jax import lax
from jax.experimental import pallas as pl
from jax.experimental.pallas import tpu as pltpu
from jax.sharding import PartitionSpec as P

MESH = pl.DeviceIdType.MESH
PRECISE = lax.Precision.HIGHEST
V_ROWS = 501
PAD_ROWS = 512
D = 3072
SLICE = 384
COUNT = (32, 48, 48)
START = (0, 32, 80)
STEP = (1, 3)
HALF = ((((0, 16), (16, 16)),) * 2, (((0, 16), (16, 32)), ((0, 32), (32, 16))))
LAUNCH = 2

SCHEDULE = (
    ((0, 0), (
        ("CX",), ("ID",), ("CY",), ("ZG",), ("SZ",), ("CZ", 0, 0, 1), ("CZ", 1, 0, 1), ("S1", 0, 0), ("S1", 0, 1),
        ("LK", 0), ("CZ", 0, 1, 1), ("CZ", 1, 1, 1), ("S1", 1, 0), ("S1", 1, 1), ("LK", 1), ("CZ", 0, 0, 2),
        ("CZ", 1, 0, 2), ("LK", 2), ("S2", 0, 0, 0), ("S2", 0, 1, 0), ("S2", 1, 0, 0), ("S2", 1, 1, 0), ("LK", 3),
        ("LS",), ("CZ", 0, 1, 2), ("CZ", 1, 1, 2), ("F1", 0, 0), ("F1", 0, 1),
    )),
    ((1, 0), (
        ("S2", 0, 0, 3), ("S2", 0, 1, 3), ("CZ", 0, 0, 3), ("CZ", 1, 0, 3), ("CZ", 0, 2, 1), ("CZ", 1, 2, 1),
        ("S2", 0, 0, 1), ("S2", 0, 1, 1), ("S2", 1, 0, 3), ("S2", 1, 1, 3), ("CZ", 0, 1, 3), ("CZ", 1, 1, 3),
        ("F1", 1, 0), ("F1", 1, 1), ("FE",),
    )),
    ((2, 0), (
        ("F2", 0, 0, 0), ("F2", 0, 1, 0), ("CZ", 0, 3, 1), ("CZ", 1, 3, 1), ("S2", 1, 0, 1), ("S2", 1, 1, 1),
        ("CZ", 0, 0, 4), ("CZ", 1, 0, 4),
    )),
    ((0, 3), (
        ("F2", 1, 0, 0), ("F2", 1, 1, 0), ("S2", 0, 0, 2), ("S2", 0, 1, 2),
    )),
    ((0, 1), (
        ("CZ", 0, 2, 2), ("CZ", 1, 2, 2), ("FW",),
    )),
    ((2, 1), (
        ("F2", 0, 0, 3), ("F2", 0, 1, 3), ("CZ", 0, 1, 4), ("CZ", 1, 1, 4), ("F2", 1, 0, 3), ("F2", 1, 1, 3),
    )),
    ((0, 2), (
        ("F2", 0, 0, 1), ("F2", 0, 1, 1), ("CZ", 0, 3, 2), ("CZ", 1, 3, 2), ("F2", 0, 0, 2), ("F2", 0, 1, 2),
    )),
    ((1, 3), (
        ("CZ", 0, 2, 3), ("CZ", 1, 2, 3), ("S2", 1, 0, 2), ("S2", 1, 1, 2),
    )),
    ((1, 1), (
        ("FIN", 0),
    )),
    ((2, 2), (
        ("CZ", 0, 3, 3), ("CZ", 1, 3, 3), ("F2", 1, 0, 1), ("F2", 1, 1, 1), ("CZ", 0, 2, 4), ("CZ", 1, 2, 4),
    )),
    ((1, 2), (
        ("F2", 1, 0, 2), ("F2", 1, 1, 2),
    )),
    ((2, 3), (
        ("CZ", 0, 3, 4), ("CZ", 1, 3, 4),
    )),
)

def logits_of(tokens, rows):
    return lax.dot_general(
        tokens, rows, (((1,), (1,)), ((), ())), preferred_element_type=jnp.float32
    )


def mix(parts):
    peaks = [part[:, 65:66] for part in parts]
    top = peaks[0]
    for peak in peaks[1:]:
        top = jnp.maximum(top, peak)
    total = parts[0] * jnp.exp(peaks[0] - top)
    for part, peak in zip(parts[1:], peaks[1:]):
        total = total + part * jnp.exp(peak - top)
    lane = lax.broadcasted_iota(jnp.int32, total.shape, 1)
    return jnp.where(lane == 65, top, total)


def total_of(parts):
    total = parts[0]
    for part in parts[1:]:
        total = total + part
    return total


def pick(step, values):
    chosen = jnp.int32(values[0])
    for number, value in enumerate(values):
        chosen = jnp.where(step == number, jnp.int32(value), chosen)
    return chosen


def kernel(
    hid_ref, grad_ref, fp_ref, vp_ref, tgt_ref, ids_ref, docs_ref, emb_ref, out_ref,
    hidv, rx, gath, hall_a, hall_bc, emb, pet, idb, part_a, part_bc, part_in_a, part_in_bc,
    look_a, look_bc, look_in_a, look_in_bc, q1_a, q1_bc, q1_in_a, q1_in_bc,
    q2, q2_in, tok, feat, side, sd_in, sz, sz_in, turned,
    sem_l, sem_c, sem_zg, sem_cx, sem_cz, sem_1, sem_2, sem_i, sem_s, sem_r, sem_q, sem_t,
):
    g, v = lax.axis_index("dp"), lax.axis_index("vocab")
    x, y = lax.rem(g, 4), lax.div(g, 4)
    z, c = lax.div(v, 2), lax.rem(v, 2)
    hall = (hall_a, hall_bc.at[0], hall_bc.at[1])
    part = (part_a, part_bc.at[0], part_bc.at[1])
    part_in = (part_in_a, part_in_bc.at[0], part_in_bc.at[1])
    look = (look_a, look_bc.at[0], look_bc.at[1])
    look_in = (look_in_a, look_in_bc.at[0], look_in_bc.at[1])
    q1 = (q1_a, q1_bc.at[0], q1_bc.at[1])
    q1_in = (q1_in_a, q1_in_bc.at[0], q1_in_bc.at[1])

    def dev(dx=0, dy=0, dz=0, dc=0):
        return (
            lax.rem(y + dy, 4) * 4 + lax.rem(x + dx, 4),
            lax.rem(z + dz, 8) * 2 + lax.rem(c + dc, 2),
        )

    def remote(src, dst, sems, at, to):
        send, recv = sems.at[(0, *at)], sems.at[(1, *at)]
        return pltpu.make_async_remote_copy(
            src_ref=src, dst_ref=dst, send_sem=send, recv_sem=recv, device_id=to, device_id_type=MESH
        )

    sent = []

    def go(copy_of, *args):
        copy_of(*args).start()
        sent.append((copy_of, args))

    def columns(zz):
        return pl.ds(pl.multiple_of(lax.rem(zz, 8) * SLICE, 128), SLICE)

    row_at, inner_at = (y, x, y), (x, y, x)

    def inner(cls, k):
        return dev(dy=k) if cls == 1 else dev(dx=k)

    def outer(cls, k):
        return dev(dx=k) if cls == 1 else dev(dy=k)

    emb_local = pltpu.make_async_copy(emb_ref, emb.at[c], sem_l.at[0])
    emb_local.start()
    barrier = pltpu.get_barrier_semaphore()
    peers = [dev(dc=1)] + [dev(dz=k) for k in range(1, 8)]
    peers += [dev(dx=k) for k in range(1, 4)] + [dev(dy=k) for k in range(1, 4)]
    for peer in peers:
        pl.semaphore_signal(barrier, inc=1, device_id=peer, device_id_type=MESH)
    first = c == 0
    hidv[...] = jnp.transpose(hid_ref[...].astype(jnp.float32)).astype(jnp.bfloat16)
    row_id = lax.broadcasted_iota(jnp.int32, (8, 128), 0)
    own_tgt = jnp.where(first, tgt_ref[0:1], tgt_ref[1:2])
    own_ids = jnp.where(first, ids_ref[0:1], ids_ref[1:2])
    idb[y, x] = jnp.where(row_id == 0, own_tgt, own_ids)
    pet[c] = jnp.zeros((128, PAD_ROWS), jnp.bfloat16)
    pet[c, :64, :V_ROWS] = vp_ref[...]
    ones_at = lax.broadcasted_iota(jnp.int32, (16, PAD_ROWS), 0) == 0
    in_table = lax.broadcasted_iota(jnp.int32, (16, PAD_ROWS), 1) < V_ROWS
    pet[c, 64:80] = jnp.where(ones_at & in_table, 1.0, 0.0).astype(jnp.bfloat16)
    pl.semaphore_wait(barrier, len(peers))

    other = pl.multiple_of((1 - c) * 128, 128)
    mine = pl.multiple_of(c * 128, 128)

    def hid_swap():
        return remote(hidv.at[pl.ds(other, 128)], rx, sem_c, (0,), dev(dc=1))

    def pet_swap():
        return remote(pet.at[c], pet.at[c], sem_c, (1,), dev(dc=1))

    def emb_swap():
        return remote(emb_ref, emb.at[c], sem_c, (2,), dev(dc=1))

    def side_swap():
        return remote(side.at[pl.ds(other, 128)], sd_in, sem_c, (3,), dev(dc=1))

    def feat_swap():
        return remote(feat.at[c], feat.at[c], sem_c, (4,), dev(dc=1))

    def tok_swap():
        return remote(tok.at[c], tok.at[c], sem_c, (5,), dev(dc=1))

    def ids_x(k):
        return remote(idb.at[y, x], idb.at[y, x], sem_i, (0, k - 1), dev(dx=k))

    def ids_y(k):
        return remote(idb.at[y], idb.at[y], sem_i, (1, k - 1), dev(dy=k))

    def along_z(k):
        block = gath.at[:, columns(z)]
        return remote(block, block, sem_zg, (k - 1,), dev(dz=k))

    def last_x(k):
        block = hall[2].at[y, x, :, columns(z)]
        return remote(block, block, sem_cx, (0, k - 1), dev(dx=k))

    def last_y(k):
        block = hall[2].at[y, :, :, columns(z)]
        return remote(block, block, sem_cx, (1, k - 1), dev(dy=k))

    def last_z(way, sub, step):
        at = columns(z + 9 - step) if way == 0 else columns(z + step - 1)
        row = lax.rem(y + sub, 4)
        cut = pl.ds(way * 2, 2) if step == 4 else slice(None)
        block = hall[2].at[row, cut, :, at]
        return remote(block, block, sem_cz, (way, sub, step - 1), dev(dz=1 if way == 0 else 7))

    def own_rows(cls):
        return gath.at[pl.ds(START[cls], COUNT[cls])]

    def first_own(cls, way):
        dst = hall[cls].at[row_at[cls], inner_at[cls]]
        return remote(own_rows(cls), dst, sem_1, (cls, way, 0), inner(cls, STEP[way]))

    def first_on(cls, way):
        pos = lax.rem(inner_at[cls] + 4 - STEP[way], 4)
        block = hall[cls].at[row_at[cls], pos, pl.ds(*HALF[cls][0][way])]
        return remote(block, block, sem_1, (cls, way, 1), inner(cls, STEP[way]))

    def second_own(cls, way, k):
        dst = hall[cls].at[row_at[cls], lax.rem(inner_at[cls] + k, 4)]
        src = own_rows(cls) if k == 0 else dst
        return remote(src, dst, sem_2, (cls, way, 0, k), outer(cls, STEP[way]))

    def second_on(cls, way, k):
        row = lax.rem(row_at[cls] + 4 - STEP[way], 4)
        block = hall[cls].at[row, lax.rem(inner_at[cls] + k, 4), pl.ds(*HALF[cls][k % 2][way])]
        return remote(block, block, sem_2, (cls, way, 1, k), outer(cls, STEP[way]))

    def side_z(k):
        to = pl.multiple_of(lax.rem(z + k, 8) * 16, 16)
        return remote(sz.at[pl.ds(to, 16)], sz_in.at[k - 1], sem_s, (0, k - 1), dev(dz=k))

    def feat_z(k):
        return remote(feat.at[c, z], feat.at[c, z], sem_s, (1, k - 1), dev(dz=k))

    def look_out(cls, k):
        return remote(
            look[cls].at[lax.rem(row_at[cls] + k, 4)], look_in[cls].at[k - 1], sem_r, (0, cls, k - 1), outer(cls, k)
        )

    def part_out(cls, k):
        return remote(part[cls].at[k], part_in[cls].at[k - 1], sem_r, (1, cls, k - 1), outer(cls, k))

    def q1_out(cls, k):
        src = q1[cls].at[lax.rem(inner_at[cls] + k, 4)]
        return remote(src, q1_in[cls].at[k - 1], sem_q, (cls, k - 1), inner(cls, k))

    def q2_out(k):
        to = pl.multiple_of(lax.rem(z + k, 8) * 16, 16)
        return remote(q2.at[pl.ds(to, 16)], q2_in.at[k - 1], sem_t, (0, k - 1), dev(dz=k))

    def tok_out(k):
        return remote(tok.at[c, z], tok.at[c, z], sem_t, (1, k - 1), dev(dz=k))

    go(hid_swap)
    for k in (1, 2, 3):
        go(ids_x, k)
    go(pet_swap)
    hid_swap().wait_recv()
    own_half, got_half = hidv[pl.ds(mine, 128), :], rx[...]
    left = jnp.where(first, own_half, got_half)
    right = jnp.where(first, got_half, own_half)
    both = jnp.concatenate([left, right], axis=1)
    hall_bc[1, y, x, :, columns(z)] = both[START[2] :]
    for k in (1, 3, 2):
        go(last_x, k)
    gath[:, columns(z)] = both[: START[2]]
    for k in (1, 7, 2, 6, 3, 5, 4):
        go(along_z, k)
    go(emb_swap)

    side_t = jnp.concatenate(
        [
            jnp.dot(fp_ref[...], hid_ref[...], preferred_element_type=jnp.float32),
            jnp.dot(fp_ref[...], grad_ref[...], preferred_element_type=jnp.float32),
        ],
        axis=0,
    )
    side[...] = jnp.transpose(side_t)
    go(side_swap)

    keep = [
        pltpu.make_async_copy(own_rows(cls), hall[cls].at[row_at[cls], inner_at[cls]], sem_l.at[1 + cls])
        for cls in (0, 1)
    ]
    row_base = (g * 16 + z * 2) * V_ROWS

    def look_up(gy, gx):
        ids = idb[gy, gx]
        wanted = jnp.concatenate([ids[0:1], ids[1:2]], axis=1) - row_base
        found = []
        for b in range(2):
            numbers = lax.broadcasted_iota(jnp.int32, (PAD_ROWS, 256), 0) + b * V_ROWS
            hit = jnp.where(numbers == wanted, 1.0, 0.0).astype(jnp.bfloat16)
            found.append(jnp.dot(pet[b, :64], hit, preferred_element_type=jnp.float32))
        found = total_of(found)
        stacked = jnp.concatenate([found[:, :128], found[:, 128:]], axis=0)
        rows = jnp.transpose(stacked).astype(jnp.bfloat16)
        look_a[gy, gx] = rows[: START[1]]
        look_bc[0, gx, gy] = rows[START[1] : START[2]]
        look_bc[1, gy, gx] = rows[START[2] :]

    arrived = set()

    def handle(what, *at):
        arrived.add((what, *at))
        if what == "CX":
            for k in (1, 2, 3):
                last_x(k).wait_recv()
            for k in (1, 3, 2):
                go(last_y, k)
        elif what == "CY":
            for k in (1, 2, 3):
                last_y(k).wait_recv()
            for sub in (0, 1):
                for way in (0, 1):
                    go(last_z, way, sub, 1)
        elif what == "CZ":
            way, sub, step = at
            last_z(way, sub, step).wait_recv()
            if step < 4:
                go(last_z, way, sub, step + 1)
            if step == LAUNCH and sub < 2:
                go(last_z, way, sub + 2, 1)
        elif what == "ZG":
            for k in range(1, 8):
                along_z(k).wait_recv()
            for cls in (0, 1):
                for way in (0, 1):
                    go(first_own, cls, way)
            for cls in (0, 1):
                for way in (0, 1):
                    go(second_own, cls, way, 0)
            for copy in keep:
                copy.start()
        elif what == "S1":
            cls, way = at
            first_own(cls, way).wait_recv()
            go(first_on, cls, way)
            for to in (0, 1):
                go(second_own, cls, to, 4 - STEP[way])
        elif what == "F1":
            cls, way = at
            first_on(cls, way).wait_recv()
            if ("F1", cls, 1 - way) in arrived:
                for to in (0, 1):
                    go(second_own, cls, to, 2)
        elif what == "S2":
            second_own(*at).wait_recv()
            go(second_on, *at)
        elif what == "F2":
            second_on(*at).wait_recv()
        elif what == "ID":
            for k in (1, 2, 3):
                ids_x(k).wait_recv()
            for k in (1, 2, 3):
                go(ids_y, k)
        elif what == "SZ":
            side_swap().wait_recv()
            sz[...] = side[pl.ds(mine, 128), :] + sd_in[...]
            for k in range(1, 8):
                go(side_z, k)
        elif what == "FE":
            for k in range(1, 8):
                side_z(k).wait_recv()
            own = sz[pl.ds(pl.multiple_of(z * 16, 16), 16), :]
            feat[c, z] = total_of([own] + [sz_in[k] for k in range(7)])
            for k in range(1, 8):
                go(feat_z, k)
        elif what == "FW":
            for k in range(1, 8):
                feat_z(k).wait_recv()
            go(feat_swap)
        elif what == "LK":
            if at[0] == 0:
                pet_swap().wait_recv()
                for k in (1, 2, 3):
                    ids_y(k).wait_recv()

            def one(gx, carry):
                look_up(at[0], gx)
                return carry

            lax.fori_loop(0, 4, one, 0)
        elif what == "LS":
            for cls in (0, 1, 2):
                for k in (1, 2, 3):
                    go(look_out, cls, k)
            emb_local.wait()
            emb_swap().wait_recv()
            for copy in keep:
                copy.wait()
        elif what == "FIN":
            (cls,) = at
            for k in (1, 2, 3):
                part_out(cls, k).wait_recv()
                look_out(cls, k).wait_recv()
            mixed = mix([part[cls][0]] + [part_in[cls][k] for k in range(3)])
            looked = total_of(
                [look[cls][row_at[cls]].astype(jnp.float32)]
                + [look_in[cls][k].astype(jnp.float32) for k in range(3)]
            )
            q1[cls][:, :, :128] = mixed.reshape(4, COUNT[cls], 128)
            q1[cls][:, :, 128:] = looked
            for k in (1, 3, 2):
                go(q1_out, cls, k)

    def partial_sums(tokens):
        logits = [logits_of(tokens, emb[b]) for b in range(2)]
        top = jnp.maximum(*[jnp.max(one, axis=1, keepdims=True) for one in logits])
        pieces = []
        for b in range(2):
            scaled = jnp.exp(logits[b] - top)
            coarse = scaled.astype(jnp.bfloat16)
            fine = (scaled - coarse.astype(jnp.float32)).astype(jnp.bfloat16)
            table = pet[b, :, :V_ROWS]
            pieces += [logits_of(coarse, table), logits_of(fine, table)]
        acc = total_of(pieces)
        lane = lax.broadcasted_iota(jnp.int32, acc.shape, 1)
        return jnp.where(lane == 65, top, acc)

    def tile(step, carry):
        for number, (_, before) in enumerate(SCHEDULE):

            @pl.when(step == number)
            def _(before=before):
                for event in before:
                    handle(*event)

        cls = pick(step, [which[0] for which, _ in SCHEDULE])
        k = pick(step, [which[1] for which, _ in SCHEDULE])

        @pl.when(cls == 0)
        def _():
            part_a[k] = partial_sums(hall_a[lax.rem(y + k, 4)].reshape(4 * COUNT[0], D))

        @pl.when(cls > 0)
        def _():
            at = jnp.where(cls == 1, x, y)
            tokens = hall_bc[cls - 1, lax.rem(at + k, 4)].reshape(4 * COUNT[1], D)
            part_bc[cls - 1, k] = partial_sums(tokens)

        for number, (which, _) in enumerate(SCHEDULE):
            if which[1] > 0:

                @pl.when(step == number)
                def _(which=which):
                    go(part_out, *which)

        return carry

    lax.fori_loop(0, len(SCHEDULE), tile, 0)

    for cls in (0, 1, 2):
        if ("FIN", cls) not in arrived:
            handle("FIN", cls)
    for cls in (0, 1, 2):
        for k in (1, 2, 3):
            q1_out(cls, k).wait_recv()
        own = q1[cls][inner_at[cls]]
        rows = slice(START[cls], START[cls] + COUNT[cls])
        q2[rows, :128] = mix([own[:, :128]] + [q1_in[cls][k, :, :128] for k in range(3)])
        q2[rows, 128:] = total_of([own[:, 128:]] + [q1_in[cls][k, :, 128:] for k in range(3)])
    for k in range(1, 8):
        go(q2_out, k)
    for k in range(1, 8):
        q2_out(k).wait_recv()
    sums = [q2[pl.ds(pl.multiple_of(z * 16, 16), 16), :]] + [q2_in[k] for k in range(7)]
    mixed = mix([one[:, :128] for one in sums])
    looked = total_of([one[:, 128:] for one in sums])
    head = mixed[:, :64] / mixed[:, 64:65] - looked[:, :64]
    tok[c, z] = jnp.concatenate([head, looked[:, 64:]], axis=1)
    for k in range(1, 8):
        go(tok_out, k)
    for k in range(1, 8):
        tok_out(k).wait_recv()
    go(tok_swap)
    feat_swap().wait_recv()
    tok_swap().wait_recv()

    for half in range(2):
        turned[half] = jnp.transpose(tok[half].reshape(128, 128))
    local = jnp.concatenate([docs_ref[0:1], docs_ref[1:2]], axis=1) - g * 4
    feats = feat[...].reshape(256, 128)
    member = [jnp.where(local == d, 1.0, 0.0) for d in range(4)]

    def products(start, right):
        left = jnp.concatenate([turned[half, pl.ds(start, 32, stride=2), :] for half in range(2)], axis=1)
        left = jnp.concatenate([left * m for m in member], axis=0)
        return jnp.dot(left, right, precision=PRECISE, preferred_element_type=jnp.float32)

    even = products(0, feats[:, :64]) + products(64, feats[:, 64:])
    odd = products(1, feats[:, :64]) + products(65, feats[:, 64:])
    result = jnp.concatenate([even, odd], axis=1)
    for d in range(4):
        out_ref[:, d, :] = result[d * 32 : d * 32 + 32]

    for copy_of, args in sent:
        copy_of(*args).wait_send()


def per_device(hidden, input_grad, embedding, vocab_proj, feature_proj, token_ids, targets, doc_ids):
    vmem = pl.BlockSpec(memory_space=pltpu.VMEM)
    bf16, f32, i32 = jnp.bfloat16, jnp.float32, jnp.int32
    dma = pltpu.SemaphoreType.DMA
    na, nb = COUNT[0], COUNT[1]
    out = pl.pallas_call(
        kernel,
        out_shape=jax.ShapeDtypeStruct((32, 4, 128), f32),
        in_specs=[vmem] * 7 + [pl.BlockSpec(memory_space=pl.ANY)],
        out_specs=vmem,
        scratch_shapes=[
            pltpu.VMEM((256, 192), bf16),
            pltpu.VMEM((128, 192), bf16),
            pltpu.VMEM((START[2], D), bf16),
            pltpu.VMEM((4, 4, na, D), bf16),
            pltpu.VMEM((2, 4, 4, nb, D), bf16),
            pltpu.VMEM((2, V_ROWS, D), bf16),
            pltpu.VMEM((2, 128, PAD_ROWS), bf16),
            pltpu.VMEM((4, 4, 8, 128), i32),
            pltpu.VMEM((4, 4 * na, 128), f32),
            pltpu.VMEM((2, 4, 4 * nb, 128), f32),
            pltpu.VMEM((3, 4 * na, 128), f32),
            pltpu.VMEM((2, 3, 4 * nb, 128), f32),
            pltpu.VMEM((4, 4, na, 128), bf16),
            pltpu.VMEM((2, 4, 4, nb, 128), bf16),
            pltpu.VMEM((3, 4, na, 128), bf16),
            pltpu.VMEM((2, 3, 4, nb, 128), bf16),
            pltpu.VMEM((4, na, 256), f32),
            pltpu.VMEM((2, 4, nb, 256), f32),
            pltpu.VMEM((3, na, 256), f32),
            pltpu.VMEM((2, 3, nb, 256), f32),
            pltpu.VMEM((128, 256), f32),
            pltpu.VMEM((7, 16, 256), f32),
            pltpu.VMEM((2, 8, 16, 128), f32),
            pltpu.VMEM((2, 8, 16, 128), f32),
            pltpu.VMEM((256, 128), f32),
            pltpu.VMEM((128, 128), f32),
            pltpu.VMEM((128, 128), f32),
            pltpu.VMEM((7, 16, 128), f32),
            pltpu.VMEM((2, 128, 128), f32),
            dma((3,)),
            dma((2, 6)),
            dma((2, 7)),
            dma((2, 2, 3)),
            dma((2, 2, 4, 4)),
            dma((2, 2, 2, 2)),
            dma((2, 2, 2, 2, 4)),
            dma((2, 2, 3)),
            dma((2, 2, 7)),
            dma((2, 2, 3, 3)),
            dma((2, 3, 3)),
            dma((2, 2, 7)),
        ],
        compiler_params=pltpu.CompilerParams(
            collective_id=0, has_side_effects=True, vmem_limit_bytes=60 * 2**20
        ),
        name="doc_grads",
    )(
        hidden.T, input_grad.T, feature_proj.T, vocab_proj.T,
        targets.reshape(2, 128), token_ids.reshape(2, 128), doc_ids.reshape(2, 128), embedding,
    )
    return out.transpose(1, 0, 2).reshape(4, 4096)


def solution(mesh):
    placed = (
        P("dp", "vocab"),
        P("dp", "vocab"),
        P(("dp", "vocab"), None),
        P(("dp", "vocab"), None),
        P("vocab", None),
        P("dp"),
        P("dp"),
        P("dp"),
    )
    return jax.shard_map(
        per_device, mesh=mesh, in_specs=placed, out_specs=P("dp", None), check_vma=False
    )
```

```python
import jax
import jax.numpy as jnp
from jax import lax
from jax.experimental import pallas as pl
from jax.experimental.pallas import tpu as pltpu
from jax.sharding import PartitionSpec as P

MESH = pl.DeviceIdType.MESH
PRECISE = lax.Precision.HIGHEST
V_ROWS = 501
PAD_ROWS = 512
D = 3072
SLICE = 384
COUNT = (32, 48, 48)
START = (0, 32, 80)
STEP = (1, 3)
HALF = ((((0, 16), (16, 16)),) * 2, (((0, 16), (16, 32)), ((0, 32), (32, 16))))
LAUNCH = 3

SCHEDULE = (
    ((1, (0,)), (
        ("ZG", 1), ("CX",), ("ID",), ("ZG", 2), ("CZ", 0, 0, 1), ("CZ", 1, 0, 1), ("ZG", 3), ("CY",),
        ("CZ", 0, 0, 2), ("CZ", 1, 0, 2), ("ZG", 4), ("SZ",), ("CZ", 1, 1, 1), ("S1", 0, 0), ("S1", 0, 1),
        ("CZ", 0, 1, 1), ("S1", 1, 0), ("S1", 1, 1), ("P2",), ("LK", 0), ("CZ", 1, 0, 3), ("CZ", 0, 0, 3), ("LK", 1),
        ("S2", 0, 0, 0), ("S2", 0, 1, 0), ("LK", 2), ("CZ", 1, 1, 2), ("S2", 1, 0, 0), ("S2", 1, 1, 0), ("LK", 3),
        ("LS",), ("CZ", 0, 1, 2), ("F1", 1, 0), ("CZ", 1, 0, 4), ("F1", 1, 1), ("CZ", 0, 0, 4),
    )),
    ((0, (0,)), (
        ("F1", 0, 0), ("F1", 0, 1), ("CZ", 1, 2, 1), ("CZ", 0, 2, 1),
    )),
    ((2, (0,)), (
        ("S2", 0, 0, 3), ("S2", 0, 1, 3), ("CZ", 1, 1, 3), ("CZ", 0, 1, 3), ("S2", 1, 0, 3), ("S2", 1, 1, 3),
        ("FE",),
    )),
    ((2, (1,)), (
        ("S2", 0, 0, 1), ("S2", 0, 1, 1), ("CZ", 1, 2, 2), ("CZ", 0, 2, 2), ("CZ", 1, 1, 4), ("CZ", 0, 1, 4),
        ("L1",),
    )),
    ((0, (1, 3)), (
        ("S2", 0, 0, 2), ("S2", 0, 1, 2), ("S2", 1, 0, 1), ("S2", 1, 1, 1), ("CZ", 1, 3, 1), ("CZ", 0, 3, 1),
        ("F2", 0, 0, 0), ("F2", 0, 1, 0),
    )),
    ((1, (1, 3)), (
        ("F2", 0, 0, 3), ("F2", 0, 1, 3), ("CZ", 1, 2, 3), ("CZ", 0, 2, 3), ("F2", 0, 0, 1), ("F2", 0, 1, 1),
        ("S2", 1, 0, 2), ("S2", 1, 1, 2),
    )),
    ((0, (2,)), (
        ("CZ", 1, 3, 2), ("CZ", 0, 3, 2), ("F2", 0, 0, 2), ("F2", 0, 1, 2), ("CZ", 1, 2, 4), ("CZ", 0, 2, 4),
        ("F2", 1, 0, 0), ("F2", 1, 1, 0), ("L2",), ("FIN", 0),
    )),
    ((2, (3,)), (
        ("F2", 1, 0, 3), ("F2", 1, 1, 3), ("FW",), ("FIN", 1),
    )),
    ((1, (2,)), (
        ("F2", 1, 0, 1), ("F2", 1, 1, 1), ("CZ", 1, 3, 3), ("CZ", 0, 3, 3), ("F2", 1, 0, 2), ("F2", 1, 1, 2),
        ("L3",),
    )),
    ((2, (2,)), (
        ("CZ", 1, 3, 4), ("CZ", 0, 3, 4), ("FIN", 2),
    )),
)


def logits_of(tokens, rows):
    return lax.dot_general(
        tokens, rows, (((1,), (1,)), ((), ())), preferred_element_type=jnp.float32
    )


def mix(parts):
    peaks = [part[:, 65:66] for part in parts]
    top = peaks[0]
    for peak in peaks[1:]:
        top = jnp.maximum(top, peak)
    total = parts[0] * jnp.exp(peaks[0] - top)
    for part, peak in zip(parts[1:], peaks[1:]):
        total = total + part * jnp.exp(peak - top)
    lane = lax.broadcasted_iota(jnp.int32, total.shape, 1)
    return jnp.where(lane == 65, top, total)


def total_of(parts):
    total = parts[0]
    for part in parts[1:]:
        total = total + part
    return total


def pick(step, values):
    chosen = jnp.int32(values[0])
    for number, value in enumerate(values):
        chosen = jnp.where(step == number, jnp.int32(value), chosen)
    return chosen


def kernel(
    hid_ref, grad_ref, fp_ref, vp_ref, tgt_ref, ids_ref, docs_ref, emb_ref, out_ref,
    hidv, rx, gath, hall_a, hall_bc, emb, pet, idb, part_a, part_bc, part_in_a, part_in_bc,
    look_a, look_bc, look_in_a, look_in_bc, look_q_a, look_q_bc, look_q_in_a, look_q_in_bc, look_z, look_z_in, found,
    far_in_a, far_in_bc, q1_a, q1_bc, q1_in_a, q1_in_bc, q2, q2_in, tok, emb_tok, feat, side, sd_in, sz, sz_in, turned,
    sem_l, sem_c, sem_zg, sem_cx, sem_cz, sem_1, sem_2, sem_i, sem_s, sem_r, sem_f, sem_q, sem_t, sem_h,
):
    g, v = lax.axis_index("dp"), lax.axis_index("vocab")
    x, y = lax.rem(g, 4), lax.div(g, 4)
    z, c = lax.div(v, 2), lax.rem(v, 2)
    hall = (hall_a, hall_bc.at[0], hall_bc.at[1])
    part = (part_a, part_bc.at[0], part_bc.at[1])
    part_in = (part_in_a, part_in_bc.at[0], part_in_bc.at[1])
    look = (look_a, look_bc.at[0], look_bc.at[1])
    look_in = (look_in_a, look_in_bc.at[0], look_in_bc.at[1])
    q1 = (q1_a, q1_bc.at[0], q1_bc.at[1])
    q1_in = (q1_in_a, q1_in_bc.at[0], q1_in_bc.at[1])
    far_in = (far_in_a, far_in_bc.at[0], far_in_bc.at[1])
    look_q = (look_q_a, look_q_bc.at[0], look_q_bc.at[1])
    look_q_in = (look_q_in_a, look_q_in_bc.at[0], look_q_in_bc.at[1])

    def dev(dx=0, dy=0, dz=0, dc=0):
        return (
            lax.rem(y + dy, 4) * 4 + lax.rem(x + dx, 4),
            lax.rem(z + dz, 8) * 2 + lax.rem(c + dc, 2),
        )

    def remote(src, dst, sems, at, to):
        send, recv = sems.at[(0, *at)], sems.at[(1, *at)]
        return pltpu.make_async_remote_copy(
            src_ref=src, dst_ref=dst, send_sem=send, recv_sem=recv, device_id=to, device_id_type=MESH
        )

    sent = []

    def go(copy_of, *args):
        copy_of(*args).start()
        sent.append((copy_of, args))

    def columns(zz):
        return pl.ds(pl.multiple_of(lax.rem(zz, 8) * SLICE, 128), SLICE)

    row_at, inner_at = (y, x, y), (x, y, x)

    def inner(cls, k):
        return dev(dy=k) if cls == 1 else dev(dx=k)

    def outer(cls, k):
        return dev(dx=k) if cls == 1 else dev(dy=k)

    emb_local = pltpu.make_async_copy(emb_ref, emb.at[c], sem_l.at[0])
    emb_local.start()
    barrier = pltpu.get_barrier_semaphore()
    peers = [dev(dc=1)] + [dev(dz=k, dc=core) for k in range(1, 8) for core in (0, 1)]
    peers += [dev(dx=k) for k in range(1, 4)] + [dev(dy=k) for k in range(1, 4)]
    peers += [dev(dx=k, dy=2) for k in (1, 2, 3)] + [dev(dx=2, dy=k) for k in (1, 3)]
    for peer in peers:
        pl.semaphore_signal(barrier, inc=1, device_id=peer, device_id_type=MESH)
    first = c == 0
    hidv[...] = jnp.transpose(hid_ref[...].astype(jnp.float32)).astype(jnp.bfloat16)
    row_id = lax.broadcasted_iota(jnp.int32, (8, 128), 0)
    own_tgt = jnp.where(first, tgt_ref[0:1], tgt_ref[1:2])
    own_ids = jnp.where(first, ids_ref[0:1], ids_ref[1:2])
    idb[y, x] = jnp.where(row_id == 0, own_tgt, own_ids)
    pet[c] = jnp.zeros((128, PAD_ROWS), jnp.bfloat16)
    pet[c, :64, :V_ROWS] = vp_ref[...]
    ones_at = lax.broadcasted_iota(jnp.int32, (16, PAD_ROWS), 0) == 0
    in_table = lax.broadcasted_iota(jnp.int32, (16, PAD_ROWS), 1) < V_ROWS
    pet[c, 64:80] = jnp.where(ones_at & in_table, 1.0, 0.0).astype(jnp.bfloat16)
    pl.semaphore_wait(barrier, len(peers))

    other = pl.multiple_of((1 - c) * 128, 128)
    mine = pl.multiple_of(c * 128, 128)

    def hid_swap():
        return remote(hidv.at[pl.ds(other, 128)], rx, sem_c, (0,), dev(dc=1))

    def pet_swap():
        return remote(pet.at[c], pet.at[c], sem_c, (1,), dev(dc=1))

    def emb_swap():
        return remote(emb_ref, emb.at[c], sem_c, (2,), dev(dc=1))

    def side_swap():
        return remote(side.at[pl.ds(other, 128)], sd_in, sem_c, (3,), dev(dc=1))

    def feat_swap():
        return remote(feat.at[c], feat.at[c], sem_c, (4,), dev(dc=1))

    def emb_tok_swap():
        return remote(emb_tok.at[c], emb_tok.at[c], sem_c, (5,), dev(dc=1))

    def ids_x(k):
        return remote(idb.at[y, x], idb.at[y, x], sem_i, (0, k - 1), dev(dx=k))

    def ids_y(k):
        return remote(idb.at[y], idb.at[y], sem_i, (1, k - 1), dev(dy=k))

    def along_z(way, step):
        at = columns(z + 9 - step) if way == 0 else columns(z + step - 1)
        block = gath.at[:, at]
        return remote(block, block, sem_zg, (way, step - 1), dev(dz=1 if way == 0 else 7))

    def last_x(k):
        block = hall[2].at[y, x, :, columns(z)]
        return remote(block, block, sem_cx, (0, k - 1), dev(dx=k))

    def last_y(k):
        block = hall[2].at[y, :, :, columns(z)]
        return remote(block, block, sem_cx, (1, k - 1), dev(dy=k))

    def last_z(way, sub, step):
        at = columns(z + 9 - step) if way == 0 else columns(z + step - 1)
        row = lax.rem(y + (0, 1, 3, 2)[sub], 4)
        cut = pl.ds(way * 2, 2) if step == 4 else slice(None)
        block = hall[2].at[row, cut, :, at]
        return remote(block, block, sem_cz, (way, sub, step - 1), dev(dz=1 if way == 0 else 7))

    def own_rows(cls):
        return gath.at[pl.ds(START[cls], COUNT[cls])]

    def first_own(cls, way):
        dst = hall[cls].at[row_at[cls], inner_at[cls]]
        return remote(own_rows(cls), dst, sem_1, (cls, way, 0), inner(cls, STEP[way]))

    def first_slice(offset):
        at = columns(z + 8 + offset)
        for cls in (0, 1):
            for way in (0, 1):
                src = gath.at[pl.ds(START[cls], COUNT[cls]), at]
                dst = hall[cls].at[row_at[cls], inner_at[cls], :, at]
                remote(src, dst, sem_1, (cls, way, 0), inner(cls, STEP[way])).start()
                if offset == 0:
                    sent.append((first_own, (cls, way)))

    def first_on(cls, way):
        pos = lax.rem(inner_at[cls] + 4 - STEP[way], 4)
        block = hall[cls].at[row_at[cls], pos, pl.ds(*HALF[cls][0][way])]
        return remote(block, block, sem_1, (cls, way, 1), inner(cls, STEP[way]))

    def second_own(cls, way, k):
        dst = hall[cls].at[row_at[cls], lax.rem(inner_at[cls] + k, 4)]
        src = own_rows(cls) if k == 0 else dst
        return remote(src, dst, sem_2, (cls, way, 0, k), outer(cls, STEP[way]))

    def second_on(cls, way, k):
        row = lax.rem(row_at[cls] + 4 - STEP[way], 4)
        block = hall[cls].at[row, lax.rem(inner_at[cls] + k, 4), pl.ds(*HALF[cls][k % 2][way])]
        return remote(block, block, sem_2, (cls, way, 1, k), outer(cls, STEP[way]))

    def side_z(k):
        to = pl.multiple_of(lax.rem(z + k, 8) * 16, 16)
        return remote(sz.at[pl.ds(to, 16)], sz_in.at[k - 1], sem_s, (0, k - 1), dev(dz=k))

    def feat_z(k):
        return remote(feat.at[c, z], feat.at[c, z], sem_s, (1, k - 1), dev(dz=k))

    def look_out(cls, k):
        return remote(
            look[cls].at[lax.rem(row_at[cls] + k, 4)], look_in[cls].at[k - 1], sem_r, (0, cls, k - 1), outer(cls, k)
        )

    def look_q_out(cls, k):
        src = look_q[cls].at[lax.rem(inner_at[cls] + k, 4)]
        return remote(src, look_q_in[cls].at[k - 1], sem_q, (1, cls, k - 1), inner(cls, k))

    def look_z_out(k):
        to = pl.multiple_of(lax.rem(z + k, 8) * 16, 16)
        return remote(look_z.at[pl.ds(to, 16)], look_z_in.at[k - 1], sem_s, (2, k - 1), dev(dz=k))

    def part_out(cls, k):
        return remote(part[cls].at[k], part_in[cls].at[k // 2], sem_r, (1, cls, k - 1), outer(cls, k))

    def far_out(cls, j):
        src = part[cls].at[2, pl.ds(pl.multiple_of(lax.rem(inner_at[cls] + j, 4) * COUNT[cls], 16), COUNT[cls])]
        to = dev(dx=2, dy=j) if cls == 1 else dev(dx=j, dy=2)
        return remote(src, far_in[cls].at[j], sem_f, (cls, j), to)

    def q1_out(cls, k):
        src = q1[cls].at[lax.rem(inner_at[cls] + k, 4)]
        return remote(src, q1_in[cls].at[k - 1], sem_q, (0, cls, k - 1), inner(cls, k))

    def q2_out(k):
        to = pl.multiple_of(lax.rem(z + k, 8) * 16, 16)
        return remote(q2.at[pl.ds(to, 16)], q2_in.at[k - 1], sem_t, (0, k - 1), dev(dz=k))

    def emb_tok_out(k):
        return remote(emb_tok.at[c, z], emb_tok.at[c, z], sem_t, (1, k - 1), dev(dz=k))

    def tok_out(k, core):
        return remote(tok.at[c, z], tok.at[c, z], sem_h, (core, k), dev(dz=k, dc=core))

    go(hid_swap)
    for k in (1, 2, 3):
        go(ids_x, k)
    go(pet_swap)
    hid_swap().wait_recv()
    own_half, got_half = hidv[pl.ds(mine, 128), :], rx[...]
    left = jnp.where(first, own_half, got_half)
    right = jnp.where(first, got_half, own_half)
    both = jnp.concatenate([left, right], axis=1)
    hall_bc[1, y, x, :, columns(z)] = both[START[2] :]
    for k in (1, 3, 2):
        go(last_x, k)
    gath[:, columns(z)] = both[: START[2]]
    for way in (0, 1):
        go(along_z, way, 1)
    first_slice(0)
    go(emb_swap)

    side_t = jnp.concatenate(
        [
            jnp.dot(fp_ref[...], hid_ref[...], preferred_element_type=jnp.float32),
            jnp.dot(fp_ref[...], grad_ref[...], preferred_element_type=jnp.float32),
        ],
        axis=0,
    )
    side[...] = jnp.transpose(side_t)
    go(side_swap)

    keep = [
        pltpu.make_async_copy(own_rows(cls), hall[cls].at[row_at[cls], inner_at[cls]], sem_l.at[1 + cls])
        for cls in (0, 1)
    ]
    row_base = (g * 16 + z * 2) * V_ROWS

    def look_up(gy, gx):
        ids = idb[gy, gx]
        wanted = jnp.concatenate([ids[0:1], ids[1:2]], axis=1) - row_base
        terms = []
        for b in range(2):
            numbers = lax.broadcasted_iota(jnp.int32, (PAD_ROWS, 256), 0) + b * V_ROWS
            hit = jnp.where(numbers == wanted, 1.0, 0.0).astype(jnp.bfloat16)
            terms.append(jnp.dot(pet[b, :64], hit, preferred_element_type=jnp.float32))
        term = total_of(terms)
        stacked = jnp.concatenate([term[:, :128], term[:, 128:]], axis=0)
        rows = jnp.transpose(stacked).astype(jnp.bfloat16)
        look_a[gy, gx] = rows[: START[1]]
        look_bc[0, gx, gy] = rows[START[1] : START[2]]
        look_bc[1, gy, gx] = rows[START[2] :]

    arrived = set()

    def handle(what, *at):
        arrived.add((what, *at))
        if what == "CX":
            for k in (1, 2, 3):
                last_x(k).wait_recv()
            for k in (1, 3, 2):
                go(last_y, k)
            for way in (0, 1):
                go(last_z, way, 0, 1)
        elif what == "CY":
            for k in (1, 2, 3):
                last_y(k).wait_recv()
            for way in (0, 1):
                go(last_z, way, 1, 1)
        elif what == "CZ":
            way, sub, step = at
            last_z(way, sub, step).wait_recv()
            if step < 4:
                go(last_z, way, sub, step + 1)
            if step == LAUNCH and sub < 2:
                go(last_z, way, sub + 2, 1)
        elif what == "ZG":
            (step,) = at
            for way in (0, 1):
                if step < 4 or way == 0:
                    along_z(way, step).wait_recv()
                if step < 3 or (step == 3 and way == 0):
                    go(along_z, way, step + 1)
            first_slice(-step)
            if step < 4:
                first_slice(step)
            else:
                for cls in (0, 1):
                    for way in (0, 1):
                        go(second_own, cls, way, 0)
                for copy in keep:
                    copy.start()
        elif what == "S1":
            cls, way = at
            first_own(cls, way).wait_recv()
            go(first_on, cls, way)
        elif what == "P2":
            for k in (3, 1):
                for cls in (0, 1):
                    for way in (0, 1):
                        go(second_own, cls, way, k)
        elif what == "F1":
            cls, way = at
            first_on(cls, way).wait_recv()
            if ("F1", cls, 1 - way) in arrived:
                for to in (0, 1):
                    go(second_own, cls, to, 2)
        elif what == "S2":
            second_own(*at).wait_recv()
            go(second_on, *at)
        elif what == "F2":
            second_on(*at).wait_recv()
        elif what == "ID":
            for k in (1, 2, 3):
                ids_x(k).wait_recv()
            for k in (1, 2, 3):
                go(ids_y, k)
        elif what == "SZ":
            side_swap().wait_recv()
            sz[...] = side[pl.ds(mine, 128), :] + sd_in[...]
            for k in range(1, 8):
                go(side_z, k)
        elif what == "FE":
            for k in range(1, 8):
                side_z(k).wait_recv()
            own = sz[pl.ds(pl.multiple_of(z * 16, 16), 16), :]
            feat[c, z] = total_of([own] + [sz_in[k] for k in range(7)])
            for k in range(1, 8):
                go(feat_z, k)
        elif what == "FW":
            for k in range(1, 8):
                feat_z(k).wait_recv()
            go(feat_swap)
        elif what == "LK":
            if at[0] == 0:
                pet_swap().wait_recv()
                for k in (1, 2, 3):
                    ids_y(k).wait_recv()

            def one(gx, carry):
                look_up(at[0], gx)
                return carry

            lax.fori_loop(0, 4, one, 0)
        elif what == "LS":
            for cls in (0, 1, 2):
                for k in (1, 2, 3):
                    go(look_out, cls, k)
            emb_local.wait()
            emb_swap().wait_recv()
            for copy in keep:
                copy.wait()
        elif what == "L1":
            for cls in (0, 1, 2):
                for k in (1, 2, 3):
                    look_out(cls, k).wait_recv()
                own = look[cls][row_at[cls]]
                look_q[cls][...] = total_of([own] + [look_in[cls][k] for k in range(3)])
                for k in (1, 2, 3):
                    go(look_q_out, cls, k)
        elif what == "L2":
            for cls in (0, 1, 2):
                for k in (1, 2, 3):
                    look_q_out(cls, k).wait_recv()
                own = look_q[cls][inner_at[cls]]
                look_z[START[cls] : START[cls] + COUNT[cls]] = total_of([own] + [look_q_in[cls][k] for k in range(3)])
            for k in range(1, 8):
                go(look_z_out, k)
        elif what == "L3":
            for k in range(1, 8):
                look_z_out(k).wait_recv()
            own = look_z[pl.ds(pl.multiple_of(z * 16, 16), 16), :]
            found[...] = total_of([one.astype(jnp.float32) for one in [own] + [look_z_in[k] for k in range(7)]])
            emb_tok[c, z] = found[...]
            for k in range(1, 8):
                go(emb_tok_out, k)
        elif what == "L4":
            for k in range(1, 8):
                emb_tok_out(k).wait_recv()
            go(emb_tok_swap)
        elif what == "FIN":
            (cls,) = at
            for k in (1, 3):
                part_out(cls, k).wait_recv()
            q1[cls][...] = mix([part[cls][0], part_in[cls][0], part_in[cls][1]]).reshape(4, COUNT[cls], 128)
            for k in (1, 3, 2):
                go(q1_out, cls, k)

    def partial_sums(tokens):
        logits = [logits_of(emb[b], tokens) for b in range(2)]
        top = jnp.maximum(*[jnp.max(one, axis=0, keepdims=True) for one in logits])
        pieces = []
        for b in range(2):
            scaled = jnp.exp(logits[b] - top)
            coarse = scaled.astype(jnp.bfloat16)
            fine = (scaled - coarse.astype(jnp.float32)).astype(jnp.bfloat16)
            table = pet[b, :, :V_ROWS]
            for piece in (coarse, fine):
                pieces.append(jnp.dot(table, piece, preferred_element_type=jnp.float32))
        acc = total_of(pieces)
        row = lax.broadcasted_iota(jnp.int32, acc.shape, 0)
        return jnp.transpose(jnp.where(row == 65, top, acc))

    def tile(step, carry):
        for number, (_, before) in enumerate(SCHEDULE):

            @pl.when(step == number)
            def _(before=before):
                for event in before:
                    handle(*event)

        cls = pick(step, [which[0] for which, _ in SCHEDULE])
        k = pick(step, [which[1][0] for which, _ in SCHEDULE])
        pair = pick(step, [len(which[1]) - 1 for which, _ in SCHEDULE])
        at = jnp.where(cls == 1, x, y)

        @pl.when((cls == 0) & (pair == 0))
        def _():
            part_a[k] = partial_sums(hall_a[lax.rem(y + k, 4)].reshape(4 * COUNT[0], D))

        @pl.when((cls > 0) & (pair == 0))
        def _():
            tokens = hall_bc[cls - 1, lax.rem(at + k, 4)].reshape(4 * COUNT[1], D)
            part_bc[cls - 1, k] = partial_sums(tokens)

        @pl.when((cls > 0) & (pair == 1))
        def _():
            rows = [hall_bc[0, lax.rem(x + near, 4)].reshape(4 * COUNT[1], D) for near in (1, 3)]
            sums = partial_sums(jnp.concatenate(rows, axis=0))
            part_bc[0, 1] = sums[: 4 * COUNT[1]]
            part_bc[0, 3] = sums[4 * COUNT[1] :]

        @pl.when((cls == 0) & (pair == 1))
        def _():
            rows = [hall_a[lax.rem(y + near, 4)].reshape(4 * COUNT[0], D) for near in (1, 3)]
            sums = partial_sums(jnp.concatenate(rows, axis=0))
            part_a[1] = sums[: 4 * COUNT[0]]
            part_a[3] = sums[4 * COUNT[0] :]

        for number, (which, _) in enumerate(SCHEDULE):
            if which[1] != (0,):

                @pl.when(step == number)
                def _(which=which):
                    for one in which[1]:
                        if one == 2:
                            for j in (2, 1, 3, 0):
                                go(far_out, which[0], j)
                        else:
                            go(part_out, which[0], one)

        return carry

    lax.fori_loop(0, len(SCHEDULE), tile, 0)

    for cls in (0, 1, 2):
        if ("FIN", cls) not in arrived:
            handle("FIN", cls)
    if ("L3",) not in arrived:
        handle("L3")
    for cls in (0, 1, 2):
        for k in (1, 2, 3):
            q1_out(cls, k).wait_recv()
        for j in range(4):
            far_out(cls, j).wait_recv()
        parts = [q1[cls][inner_at[cls]]] + [q1_in[cls][k] for k in range(3)] + [far_in[cls][j] for j in range(4)]
        q2[START[cls] : START[cls] + COUNT[cls]] = mix(parts)
    for k in (4, 3, 5, 2, 6, 1, 7):
        go(q2_out, k)
    handle("L4")
    for k in range(1, 8):
        q2_out(k).wait_recv()
    mixed = mix([q2[pl.ds(pl.multiple_of(z * 16, 16), 16), :]] + [q2_in[k] for k in range(7)])
    head = mixed[:, :64] / mixed[:, 64:65] - found[:, :64]
    tok[c, z] = jnp.concatenate([head[:8], head[8:]], axis=1)
    others = [(k, core) for k in (4, 3, 5, 2, 6, 1, 7, 0) for core in (0, 1) if (k, core) != (0, 0)]
    for k, core in others:
        go(tok_out, k, core)
    feat_swap().wait_recv()
    emb_tok_swap().wait_recv()
    feats = feat[...].reshape(256, 128)
    local = jnp.concatenate([docs_ref[0:1], docs_ref[1:2]], axis=1) - g * 4
    member = [jnp.where(local == d, 1.0, 0.0) for d in range(4)]

    def products(start, right):
        left = jnp.concatenate([turned[half, pl.ds(start, 32, stride=2), :] for half in range(2)], axis=1)
        left = jnp.concatenate([left * m for m in member], axis=0)
        return jnp.dot(left, right, precision=PRECISE, preferred_element_type=jnp.float32)

    for half in range(2):
        turned[half] = jnp.transpose(emb_tok[half].reshape(128, 128))
    even = products(64, feats[:, 64:])
    odd = products(65, feats[:, 64:])
    for k, core in others:
        tok_out(k, core).wait_recv()

    for half in range(2):
        rows = [tok[half, :, :, 64 * side : 64 * side + 64].reshape(8, 1, 8, 64) for side in range(2)]
        heads = jnp.concatenate(rows, axis=1).reshape(128, 64)
        turned[half, :64] = jnp.transpose(heads)
    even = even + products(0, feats[:, :64])
    odd = odd + products(1, feats[:, :64])
    result = jnp.concatenate([even, odd], axis=1)
    for d in range(4):
        out_ref[:, d, :] = result[d * 32 : d * 32 + 32]

    for copy_of, args in sent:
        copy_of(*args).wait_send()


def per_device(hidden, input_grad, embedding, vocab_proj, feature_proj, token_ids, targets, doc_ids):
    vmem = pl.BlockSpec(memory_space=pltpu.VMEM)
    bf16, f32, i32 = jnp.bfloat16, jnp.float32, jnp.int32
    dma = pltpu.SemaphoreType.DMA
    na, nb = COUNT[0], COUNT[1]
    out = pl.pallas_call(
        kernel,
        out_shape=jax.ShapeDtypeStruct((32, 4, 128), f32),
        in_specs=[vmem] * 7 + [pl.BlockSpec(memory_space=pl.ANY)],
        out_specs=vmem,
        scratch_shapes=[
            pltpu.VMEM((256, 192), bf16),
            pltpu.VMEM((128, 192), bf16),
            pltpu.VMEM((START[2], D), bf16),
            pltpu.VMEM((4, 4, na, D), bf16),
            pltpu.VMEM((2, 4, 4, nb, D), bf16),
            pltpu.VMEM((2, V_ROWS, D), bf16),
            pltpu.VMEM((2, 128, PAD_ROWS), bf16),
            pltpu.VMEM((4, 4, 8, 128), i32),
            pltpu.VMEM((4, 4 * na, 128), f32),
            pltpu.VMEM((2, 4, 4 * nb, 128), f32),
            pltpu.VMEM((2, 4 * na, 128), f32),
            pltpu.VMEM((2, 2, 4 * nb, 128), f32),
            pltpu.VMEM((4, 4, na, 128), bf16),
            pltpu.VMEM((2, 4, 4, nb, 128), bf16),
            pltpu.VMEM((3, 4, na, 128), bf16),
            pltpu.VMEM((2, 3, 4, nb, 128), bf16),
            pltpu.VMEM((4, na, 128), bf16),
            pltpu.VMEM((2, 4, nb, 128), bf16),
            pltpu.VMEM((3, na, 128), bf16),
            pltpu.VMEM((2, 3, nb, 128), bf16),
            pltpu.VMEM((128, 128), bf16),
            pltpu.VMEM((7, 16, 128), bf16),
            pltpu.VMEM((16, 128), f32),
            pltpu.VMEM((4, na, 128), f32),
            pltpu.VMEM((2, 4, nb, 128), f32),
            pltpu.VMEM((4, na, 128), f32),
            pltpu.VMEM((2, 4, nb, 128), f32),
            pltpu.VMEM((3, na, 128), f32),
            pltpu.VMEM((2, 3, nb, 128), f32),
            pltpu.VMEM((128, 128), f32),
            pltpu.VMEM((7, 16, 128), f32),
            pltpu.VMEM((2, 8, 8, 128), f32),
            pltpu.VMEM((2, 8, 16, 128), f32),
            pltpu.VMEM((2, 8, 16, 128), f32),
            pltpu.VMEM((256, 128), f32),
            pltpu.VMEM((128, 128), f32),
            pltpu.VMEM((128, 128), f32),
            pltpu.VMEM((7, 16, 128), f32),
            pltpu.VMEM((2, 128, 128), f32),
            dma((3,)),
            dma((2, 6)),
            dma((2, 2, 4)),
            dma((2, 2, 3)),
            dma((2, 2, 4, 4)),
            dma((2, 2, 2, 2)),
            dma((2, 2, 2, 2, 4)),
            dma((2, 2, 3)),
            dma((2, 3, 7)),
            dma((2, 2, 3, 3)),
            dma((2, 3, 4)),
            dma((2, 2, 3, 3)),
            dma((2, 2, 7)),
            dma((2, 2, 8)),
        ],
        compiler_params=pltpu.CompilerParams(
            collective_id=0, has_side_effects=True, vmem_limit_bytes=60 * 2**20
        ),
        name="doc_grads",
    )(
        hidden.T, input_grad.T, feature_proj.T, vocab_proj.T,
        targets.reshape(2, 128), token_ids.reshape(2, 128), doc_ids.reshape(2, 128), embedding,
    )
    return out.transpose(1, 0, 2).reshape(4, 4096)


def solution(mesh):
    placed = (
        P("dp", "vocab"),
        P("dp", "vocab"),
        P(("dp", "vocab"), None),
        P(("dp", "vocab"), None),
        P("vocab", None),
        P("dp"),
        P("dp"),
        P("dp"),
    )
    return jax.shard_map(
        per_device, mesh=mesh, in_specs=placed, out_specs=P("dp", None), check_vma=False
    )
```

```python
import jax
import jax.numpy as jnp
from jax import lax
from jax.experimental import pallas as pl
from jax.experimental.pallas import tpu as pltpu
from jax.sharding import PartitionSpec as P

MESH = pl.DeviceIdType.MESH
PRECISE = lax.Precision.HIGHEST
V_ROWS = 501
PAD_ROWS = 512
D = 3072
SLICE = 384
COUNT = (32, 48, 48)
START = (0, 32, 80)
STEP = (1, 3)
HALF = ((((0, 16), (16, 16)),) * 2, (((0, 16), (16, 32)), ((0, 32), (32, 16))))
LAUNCH = 2

SCHEDULE = (
    ((1, 0, 0, 0), (
        ("ZG", 1), ("CX",), ("ID",), ("ZG", 2), ("CZ", 0, 0, 1), ("CZ", 1, 0, 1), ("ZG", 3), ("CY", 2), ("CY", 1),
        ("CY", 3), ("CZ", 0, 0, 2), ("CZ", 1, 0, 2), ("ZG", 4), ("SZ",), ("CZ", 1, 1, 1), ("S1", 0, 0), ("S1", 0, 1),
        ("CZ", 0, 1, 1), ("S2", 1, 0, 0), ("S2", 1, 1, 0), ("S1", 1, 0), ("S1", 1, 1), ("P2",), ("LK", 0),
        ("S2", 0, 0, 0), ("LK", 1), ("S2", 0, 1, 0), ("LK", 2), ("CZ", 1, 0, 3), ("CZ", 0, 0, 3), ("F1", 0, 0),
        ("LK", 3), ("LS",), ("F1", 0, 1), ("CZ", 1, 2, 1), ("CZ", 0, 2, 1), ("F1", 1, 0), ("F1", 1, 1),
    )),
    ((2, 0, 0, 1), (
        ("F2", 1, 0, 0), ("F2", 1, 1, 0), ("CZ", 1, 1, 2), ("CZ", 0, 1, 2), ("CZ", 1, 0, 4), ("S2", 0, 0, 3),
        ("S2", 0, 1, 3), ("CZ", 0, 0, 4),
    )),
    ((2, 1, 1, 0), (
        ("CZ", 1, 2, 2), ("S2", 1, 0, 3), ("S2", 1, 1, 3), ("CZ", 0, 2, 2), ("S2", 0, 0, 1), ("S2", 0, 1, 1),
        ("CZ", 1, 1, 3), ("F2", 0, 0, 0), ("F2", 0, 1, 0), ("CZ", 0, 1, 3), ("CZ", 1, 3, 1), ("S2", 1, 0, 1),
        ("S2", 1, 1, 1), ("CZ", 0, 3, 1), ("S2", 0, 0, 2), ("S2", 0, 1, 2), ("CZ", 1, 2, 3), ("F2", 0, 0, 3),
        ("F2", 0, 1, 3), ("CZ", 0, 2, 3), ("CZ", 1, 1, 4), ("CZ", 0, 1, 4), ("F2", 0, 0, 1),
    )),
    ((1, 1, 1, 1), (
        ("F2", 0, 1, 1), ("S2", 1, 0, 2), ("S2", 1, 1, 2), ("CZ", 1, 3, 2), ("F2", 0, 0, 2), ("F2", 0, 1, 2),
        ("CZ", 0, 3, 2),
    )),
    ((1, 3, 3, 0), (
        ("CZ", 1, 2, 4), ("F2", 1, 0, 3), ("F2", 1, 1, 3), ("CZ", 0, 2, 4), ("FE",),
    )),
    ((2, 3, 3, 1), (
        ("F2", 1, 0, 1), ("F2", 1, 1, 1), ("CZ", 1, 3, 3), ("CZ", 0, 3, 3), ("L1",),
    )),
    ((1, 2, 2, 0), (
        ("F2", 1, 0, 2), ("F2", 1, 1, 2),
    )),
    ((2, 2, 2, 1), (
        ("CZ", 1, 3, 4), ("CZ", 0, 3, 4), ("L2",), ("FW",), ("FIN", 1),
    )),
)


def logits_of(tokens, rows):
    return lax.dot_general(
        tokens, rows, (((1,), (1,)), ((), ())), preferred_element_type=jnp.float32
    )


def mix(parts):
    peaks = [part[:, 65:66] for part in parts]
    top = peaks[0]
    for peak in peaks[1:]:
        top = jnp.maximum(top, peak)
    total = parts[0] * jnp.exp(peaks[0] - top)
    for part, peak in zip(parts[1:], peaks[1:]):
        total = total + part * jnp.exp(peak - top)
    lane = lax.broadcasted_iota(jnp.int32, total.shape, 1)
    return jnp.where(lane == 65, top, total)


def total_of(parts):
    total = parts[0]
    for part in parts[1:]:
        total = total + part
    return total


def pick(step, values):
    chosen = jnp.int32(values[0])
    for number, value in enumerate(values):
        chosen = jnp.where(step == number, jnp.int32(value), chosen)
    return chosen


def kernel(
    hid_ref, grad_ref, fp_ref, vp_ref, tgt_ref, ids_ref, docs_ref, emb_ref, out_ref,
    hidv, rx, gath, hall_a, hall_bc, emb, pet, idb, part_a, part_bc, part_in_a, part_in_bc,
    look_a, look_bc, look_in_a, look_in_bc, look_q_a, look_q_bc, look_q_in_a, look_q_in_bc, look_z, look_z_in, found,
    far_in_a, far_in_bc, q1_a, q1_bc, q1_in_a, q1_in_bc, q2, q2_in, tok, emb_tok, feat, side, sd_in, sz, sz_in, turned,
    sem_l, sem_c, sem_zg, sem_cx, sem_cz, sem_1, sem_2, sem_i, sem_s, sem_r, sem_f, sem_q, sem_t, sem_h,
):
    g, v = lax.axis_index("dp"), lax.axis_index("vocab")
    x, y = lax.rem(g, 4), lax.div(g, 4)
    z, c = lax.div(v, 2), lax.rem(v, 2)
    hall = (hall_a, hall_bc.at[0], hall_bc.at[1])
    part = (part_a, part_bc.at[0], part_bc.at[1])
    part_in = (part_in_a, part_in_bc.at[0], part_in_bc.at[1])
    look = (look_a, look_bc.at[0], look_bc.at[1])
    look_in = (look_in_a, look_in_bc.at[0], look_in_bc.at[1])
    q1 = (q1_a, q1_bc.at[0], q1_bc.at[1])
    q1_in = (q1_in_a, q1_in_bc.at[0], q1_in_bc.at[1])
    far_in = (far_in_a, far_in_bc.at[0], far_in_bc.at[1])
    look_q = (look_q_a, look_q_bc.at[0], look_q_bc.at[1])
    look_q_in = (look_q_in_a, look_q_in_bc.at[0], look_q_in_bc.at[1])

    def dev(dx=0, dy=0, dz=0, dc=0):
        return (
            lax.rem(y + dy, 4) * 4 + lax.rem(x + dx, 4),
            lax.rem(z + dz, 8) * 2 + lax.rem(c + dc, 2),
        )

    def remote(src, dst, sems, at, to):
        send, recv = sems.at[(0, *at)], sems.at[(1, *at)]
        return pltpu.make_async_remote_copy(
            src_ref=src, dst_ref=dst, send_sem=send, recv_sem=recv, device_id=to, device_id_type=MESH
        )

    sent = []

    def go(copy_of, *args):
        copy_of(*args).start()
        sent.append((copy_of, args))

    def columns(zz):
        return pl.ds(pl.multiple_of(lax.rem(zz, 8) * SLICE, 128), SLICE)

    row_at, inner_at = (y, x, y), (x, y, x)

    def inner(cls, k):
        return dev(dy=k) if cls == 1 else dev(dx=k)

    def outer(cls, k):
        return dev(dx=k) if cls == 1 else dev(dy=k)

    emb_local = pltpu.make_async_copy(emb_ref, emb.at[c], sem_l.at[0])
    emb_local.start()
    barrier = pltpu.get_barrier_semaphore()
    peers = [dev(dc=1)] + [dev(dz=k, dc=core) for k in range(1, 8) for core in (0, 1)]
    peers += [dev(dx=k) for k in range(1, 4)] + [dev(dy=k) for k in range(1, 4)]
    peers += [dev(dx=k, dy=2) for k in (1, 2, 3)] + [dev(dx=2, dy=k) for k in (1, 3)]
    for peer in peers:
        pl.semaphore_signal(barrier, inc=1, device_id=peer, device_id_type=MESH)
    first = c == 0
    hidv[...] = jnp.transpose(hid_ref[...].astype(jnp.float32)).astype(jnp.bfloat16)
    row_id = lax.broadcasted_iota(jnp.int32, (8, 128), 0)
    own_tgt = jnp.where(first, tgt_ref[0:1], tgt_ref[1:2])
    own_ids = jnp.where(first, ids_ref[0:1], ids_ref[1:2])
    idb[y, x] = jnp.where(row_id == 0, own_tgt, own_ids)
    pet[c] = jnp.zeros((128, PAD_ROWS), jnp.bfloat16)
    pet[c, :64, :V_ROWS] = vp_ref[...]
    ones_at = lax.broadcasted_iota(jnp.int32, (16, PAD_ROWS), 0) == 0
    in_table = lax.broadcasted_iota(jnp.int32, (16, PAD_ROWS), 1) < V_ROWS
    pet[c, 64:80] = jnp.where(ones_at & in_table, 1.0, 0.0).astype(jnp.bfloat16)
    pl.semaphore_wait(barrier, len(peers))

    other = pl.multiple_of((1 - c) * 128, 128)
    mine = pl.multiple_of(c * 128, 128)

    def hid_swap():
        return remote(hidv.at[pl.ds(other, 128)], rx, sem_c, (0,), dev(dc=1))

    def pet_swap():
        return remote(pet.at[c], pet.at[c], sem_c, (1,), dev(dc=1))

    def emb_swap():
        return remote(emb_ref, emb.at[c], sem_c, (2,), dev(dc=1))

    def side_swap():
        return remote(side.at[pl.ds(other, 128)], sd_in, sem_c, (3,), dev(dc=1))

    def feat_swap():
        return remote(feat.at[c], feat.at[c], sem_c, (4,), dev(dc=1))

    def emb_tok_swap():
        return remote(emb_tok.at[c], emb_tok.at[c], sem_c, (5,), dev(dc=1))

    def ids_x(k):
        return remote(idb.at[y, x], idb.at[y, x], sem_i, (0, k - 1), dev(dx=k))

    def ids_y(k):
        return remote(idb.at[y], idb.at[y], sem_i, (1, k - 1), dev(dy=k))

    def along_z(way, step):
        at = columns(z + 9 - step) if way == 0 else columns(z + step - 1)
        block = gath.at[:, at]
        return remote(block, block, sem_zg, (way, step - 1), dev(dz=1 if way == 0 else 7))

    def last_x(k):
        block = hall[2].at[y, x, :, columns(z)]
        return remote(block, block, sem_cx, (0, k - 1), dev(dx=k))

    def last_y(k):
        block = hall[2].at[y, :, :, columns(z)]
        return remote(block, block, sem_cx, (1, k - 1), dev(dy=k))

    def last_z(way, sub, step):
        at = columns(z + 9 - step) if way == 0 else columns(z + step - 1)
        row = lax.rem(y + (0, 1, 3, 2)[sub], 4)
        cut = pl.ds(way * 2, 2) if step == 4 else slice(None)
        block = hall[2].at[row, cut, :, at]
        return remote(block, block, sem_cz, (way, sub, step - 1), dev(dz=1 if way == 0 else 7))

    def own_rows(cls):
        return gath.at[pl.ds(START[cls], COUNT[cls])]

    def first_own(cls, way):
        dst = hall[cls].at[row_at[cls], inner_at[cls]]
        return remote(own_rows(cls), dst, sem_1, (cls, way, 0), inner(cls, STEP[way]))

    def first_slice(offset):
        at = columns(z + 8 + offset)
        for cls in (0, 1):
            for way in (0, 1):
                src = gath.at[pl.ds(START[cls], COUNT[cls]), at]
                dst = hall[cls].at[row_at[cls], inner_at[cls], :, at]
                remote(src, dst, sem_1, (cls, way, 0), inner(cls, STEP[way])).start()
                remote(src, dst, sem_2, (cls, way, 0, 0), outer(cls, STEP[way])).start()
                if offset == 0:
                    sent.append((first_own, (cls, way)))
                    sent.append((second_own, (cls, way, 0)))

    def first_on(cls, way):
        pos = lax.rem(inner_at[cls] + 4 - STEP[way], 4)
        block = hall[cls].at[row_at[cls], pos, pl.ds(*HALF[cls][0][way])]
        return remote(block, block, sem_1, (cls, way, 1), inner(cls, STEP[way]))

    def second_own(cls, way, k):
        dst = hall[cls].at[row_at[cls], lax.rem(inner_at[cls] + k, 4)]
        src = own_rows(cls) if k == 0 else dst
        return remote(src, dst, sem_2, (cls, way, 0, k), outer(cls, STEP[way]))

    def second_on(cls, way, k):
        row = lax.rem(row_at[cls] + 4 - STEP[way], 4)
        block = hall[cls].at[row, lax.rem(inner_at[cls] + k, 4), pl.ds(*HALF[cls][k % 2][way])]
        return remote(block, block, sem_2, (cls, way, 1, k), outer(cls, STEP[way]))

    def side_z(k):
        to = pl.multiple_of(lax.rem(z + k, 8) * 16, 16)
        return remote(sz.at[pl.ds(to, 16)], sz_in.at[k - 1], sem_s, (0, k - 1), dev(dz=k))

    def feat_z(k):
        return remote(feat.at[c, z], feat.at[c, z], sem_s, (1, k - 1), dev(dz=k))

    def look_out(cls, k):
        return remote(
            look[cls].at[lax.rem(row_at[cls] + k, 4)], look_in[cls].at[k - 1], sem_r, (0, cls, k - 1), outer(cls, k)
        )

    def look_q_out(cls, k):
        src = look_q[cls].at[lax.rem(inner_at[cls] + k, 4)]
        return remote(src, look_q_in[cls].at[k - 1], sem_q, (1, cls, k - 1), inner(cls, k))

    def look_z_out(k):
        to = pl.multiple_of(lax.rem(z + k, 8) * 16, 16)
        return remote(look_z.at[pl.ds(to, 16)], look_z_in.at[k - 1], sem_s, (2, k - 1), dev(dz=k))

    def part_out(cls, k):
        return remote(part[cls].at[k], part_in[cls].at[k // 2], sem_r, (1, cls, k - 1), outer(cls, k))

    def far_out(cls, j):
        src = part[cls].at[2, pl.ds(pl.multiple_of(lax.rem(inner_at[cls] + j, 4) * COUNT[cls], 16), COUNT[cls])]
        to = dev(dx=2, dy=j) if cls == 1 else dev(dx=j, dy=2)
        return remote(src, far_in[cls].at[j], sem_f, (cls, j), to)

    def q1_out(cls, k):
        src = q1[cls].at[lax.rem(inner_at[cls] + k, 4)]
        return remote(src, q1_in[cls].at[k - 1], sem_q, (0, cls, k - 1), inner(cls, k))

    def q2_out(k):
        to = pl.multiple_of(lax.rem(z + k, 8) * 16, 16)
        return remote(q2.at[pl.ds(to, 16)], q2_in.at[k - 1], sem_t, (0, k - 1), dev(dz=k))

    def emb_tok_out(k):
        return remote(emb_tok.at[c, z], emb_tok.at[c, z], sem_t, (1, k - 1), dev(dz=k))

    def tok_out(k, core):
        return remote(tok.at[c, z], tok.at[c, z], sem_h, (core, k), dev(dz=k, dc=core))

    go(hid_swap)
    for k in (1, 2, 3):
        go(ids_x, k)
    go(pet_swap)
    hid_swap().wait_recv()
    own_half, got_half = hidv[pl.ds(mine, 128), :], rx[...]
    left = jnp.where(first, own_half, got_half)
    right = jnp.where(first, got_half, own_half)
    both = jnp.concatenate([left, right], axis=1)
    hall_bc[1, y, x, :, columns(z)] = both[START[2] :]
    for k in (1, 3, 2):
        go(last_x, k)
    gath[:, columns(z)] = both[: START[2]]
    for way in (0, 1):
        go(along_z, way, 1)
    first_slice(0)
    go(emb_swap)

    side_t = jnp.concatenate(
        [
            jnp.dot(fp_ref[...], hid_ref[...], preferred_element_type=jnp.float32),
            jnp.dot(fp_ref[...], grad_ref[...], preferred_element_type=jnp.float32),
        ],
        axis=0,
    )
    side[...] = jnp.transpose(side_t)
    go(side_swap)

    keep = [
        pltpu.make_async_copy(own_rows(cls), hall[cls].at[row_at[cls], inner_at[cls]], sem_l.at[1 + cls])
        for cls in (0, 1)
    ]
    row_base = (g * 16 + z * 2) * V_ROWS

    def look_up(gy, gx):
        ids = idb[gy, gx]
        wanted = jnp.concatenate([ids[0:1], ids[1:2]], axis=1) - row_base
        terms = []
        for b in range(2):
            numbers = lax.broadcasted_iota(jnp.int32, (PAD_ROWS, 256), 0) + b * V_ROWS
            hit = jnp.where(numbers == wanted, 1.0, 0.0).astype(jnp.bfloat16)
            terms.append(jnp.dot(pet[b, :64], hit, preferred_element_type=jnp.float32))
        term = total_of(terms)
        stacked = jnp.concatenate([term[:, :128], term[:, 128:]], axis=0)
        rows = jnp.transpose(stacked).astype(jnp.bfloat16)
        look_a[gy, gx] = rows[: START[1]]
        look_bc[0, gx, gy] = rows[START[1] : START[2]]
        look_bc[1, gy, gx] = rows[START[2] :]

    arrived, held = set(), {}

    def handle(what, *at):
        arrived.add((what, *at))
        if what == "CX":
            for k in (1, 2, 3):
                last_x(k).wait_recv()
            for k in (3, 1, 2):
                go(last_y, k)
            for way in (0, 1):
                go(last_z, way, 0, 1)
        elif what == "CY":
            (sub,) = at
            last_y(4 - (0, 1, 3, 2)[sub]).wait_recv()
            if sub == 1:
                for way in (0, 1):
                    go(last_z, way, 1, 1)
        elif what == "CZ":
            way, sub, step = at
            last_z(way, sub, step).wait_recv()
            if step < 4:
                go(last_z, way, sub, step + 1)
            if step == LAUNCH and sub < 2:
                go(last_z, way, sub + 2, 1)
        elif what == "ZG":
            (step,) = at
            for way in (0, 1):
                if step < 4 or way == 0:
                    along_z(way, step).wait_recv()
                if step < 3 or (step == 3 and way == 0):
                    go(along_z, way, step + 1)
            first_slice(-step)
            if step < 4:
                first_slice(step)
            else:
                for copy in keep:
                    copy.start()
        elif what == "S1":
            cls, way = at
            first_own(cls, way).wait_recv()
            go(first_on, cls, way)
        elif what == "P2":
            for k in (3, 1):
                for cls in (0, 1):
                    for way in (0, 1):
                        go(second_own, cls, way, k)
        elif what == "F1":
            cls, way = at
            first_on(cls, way).wait_recv()
            if ("F1", cls, 1 - way) in arrived:
                for to in (0, 1):
                    go(second_own, cls, to, 2)
                for block in held.pop(cls, ()):
                    go(second_on, *block)
        elif what == "S2":
            second_own(*at).wait_recv()
            if True:
                go(second_on, *at)
            else:
                held.setdefault(at[0], []).append(at)
        elif what == "F2":
            second_on(*at).wait_recv()
        elif what == "ID":
            for k in (1, 2, 3):
                ids_x(k).wait_recv()
            for k in (1, 2, 3):
                go(ids_y, k)
        elif what == "SZ":
            side_swap().wait_recv()
            sz[...] = side[pl.ds(mine, 128), :] + sd_in[...]
            for k in range(1, 8):
                go(side_z, k)
        elif what == "FE":
            for k in range(1, 8):
                side_z(k).wait_recv()
            own = sz[pl.ds(pl.multiple_of(z * 16, 16), 16), :]
            feat[c, z] = total_of([own] + [sz_in[k] for k in range(7)])
            for k in range(1, 8):
                go(feat_z, k)
        elif what == "FW":
            for k in range(1, 8):
                feat_z(k).wait_recv()
            go(feat_swap)
        elif what == "LK":
            if at[0] == 0:
                pet_swap().wait_recv()
                for k in (1, 2, 3):
                    ids_y(k).wait_recv()

            def one(gx, carry):
                look_up(at[0], gx)
                return carry

            lax.fori_loop(0, 4, one, 0)
        elif what == "LS":
            for cls in (0, 1, 2):
                for k in (1, 2, 3):
                    go(look_out, cls, k)
            emb_local.wait()
            emb_swap().wait_recv()
            for copy in keep:
                copy.wait()
        elif what == "L1":
            for cls in (0, 1, 2):
                for k in (1, 2, 3):
                    look_out(cls, k).wait_recv()
                own = look[cls][row_at[cls]]
                look_q[cls][...] = total_of([own] + [look_in[cls][k] for k in range(3)])
                for k in (1, 2, 3):
                    go(look_q_out, cls, k)
        elif what == "L2":
            for cls in (0, 1, 2):
                for k in (1, 2, 3):
                    look_q_out(cls, k).wait_recv()
                own = look_q[cls][inner_at[cls]]
                look_z[START[cls] : START[cls] + COUNT[cls]] = total_of([own] + [look_q_in[cls][k] for k in range(3)])
            for k in range(1, 8):
                go(look_z_out, k)
        elif what == "L3":
            for k in range(1, 8):
                look_z_out(k).wait_recv()
            own = look_z[pl.ds(pl.multiple_of(z * 16, 16), 16), :]
            found[...] = total_of([one.astype(jnp.float32) for one in [own] + [look_z_in[k] for k in range(7)]])
            emb_tok[c, z] = found[...]
            for k in range(1, 8):
                go(emb_tok_out, k)
        elif what == "L4":
            for k in range(1, 8):
                emb_tok_out(k).wait_recv()
            go(emb_tok_swap)
        elif what == "FIN":
            (cls,) = at
            for k in (1, 3):
                part_out(cls, k).wait_recv()
            q1[cls][...] = mix([part[cls][0], part_in[cls][0], part_in[cls][1]]).reshape(4, COUNT[cls], 128)
            for k in (1, 3, 2):
                go(q1_out, cls, k)

    def partial_sums(tokens):
        logits = [logits_of(emb[b], tokens) for b in range(2)]
        top = jnp.maximum(*[jnp.max(one, axis=0, keepdims=True) for one in logits])
        pieces = []
        for b in range(2):
            scaled = jnp.exp(logits[b] - top)
            coarse = scaled.astype(jnp.bfloat16)
            fine = (scaled - coarse.astype(jnp.float32)).astype(jnp.bfloat16)
            table = pet[b, :, :V_ROWS]
            for piece in (coarse, fine):
                pieces.append(jnp.dot(table, piece, preferred_element_type=jnp.float32))
        acc = total_of(pieces)
        row = lax.broadcasted_iota(jnp.int32, acc.shape, 0)
        return jnp.transpose(jnp.where(row == 65, top, acc))

    def tile(step, carry):
        for number, (_, before) in enumerate(SCHEDULE):

            @pl.when(step == number)
            def _(before=before):
                for event in before:
                    handle(*event)

        cls, k, near, half = [pick(step, [which[n] for which, _ in SCHEDULE]) for n in range(4)]
        row = lax.rem(jnp.where(cls == 1, x, y) + k, 4)
        tokens = hall_bc[cls - 1, row].reshape(4 * COUNT[1], D)
        beside = hall_a[lax.rem(y + near, 4), pl.ds(half * 2, 2)].reshape(2 * COUNT[0], D)
        sums = partial_sums(jnp.concatenate([tokens, beside], axis=0))
        part_bc[cls - 1, k] = sums[: 4 * COUNT[1]]
        at = pl.multiple_of(half * 2 * COUNT[0], 2 * COUNT[0])
        part_a[near, pl.ds(at, 2 * COUNT[0])] = sums[4 * COUNT[1] :]

        for number, (which, _) in enumerate(SCHEDULE):

            @pl.when(step == number)
            def _(which=which):
                for one, turn in ((which[0], which[1]), (0, which[2])):
                    if one == 0 and which[3] == 0:
                        continue
                    if turn == 2:
                        for j in (2, 1, 3, 0):
                            go(far_out, one, j)
                    elif turn > 0:
                        go(part_out, one, turn)

        return carry

    lax.fori_loop(0, len(SCHEDULE), tile, 0)

    for cls in (0, 1, 2):
        if ("FIN", cls) not in arrived:
            handle("FIN", cls)
    if ("L3",) not in arrived:
        handle("L3")
    for cls in (0, 1, 2):
        for k in (1, 2, 3):
            q1_out(cls, k).wait_recv()
        for j in range(4):
            far_out(cls, j).wait_recv()
        parts = [q1[cls][inner_at[cls]]] + [q1_in[cls][k] for k in range(3)] + [far_in[cls][j] for j in range(4)]
        q2[START[cls] : START[cls] + COUNT[cls]] = mix(parts)
    for k in (4, 3, 5, 2, 6, 1, 7):
        go(q2_out, k)
    handle("L4")
    for k in range(1, 8):
        q2_out(k).wait_recv()
    mixed = mix([q2[pl.ds(pl.multiple_of(z * 16, 16), 16), :]] + [q2_in[k] for k in range(7)])
    head = mixed[:, :64] / mixed[:, 64:65] - found[:, :64]
    tok[c, z] = jnp.concatenate([head[:8], head[8:]], axis=1)
    others = [(k, core) for k in (4, 3, 5, 2, 6, 1, 7, 0) for core in (0, 1) if (k, core) != (0, 0)]
    for k, core in others:
        go(tok_out, k, core)
    feat_swap().wait_recv()
    emb_tok_swap().wait_recv()
    feats = feat[...].reshape(256, 128)
    local = jnp.concatenate([docs_ref[0:1], docs_ref[1:2]], axis=1) - g * 4
    member = [jnp.where(local == d, 1.0, 0.0) for d in range(4)]

    def products(start, right):
        left = jnp.concatenate([turned[half, pl.ds(start, 32, stride=2), :] for half in range(2)], axis=1)
        left = jnp.concatenate([left * m for m in member], axis=0)
        return jnp.dot(left, right, precision=PRECISE, preferred_element_type=jnp.float32)

    for half in range(2):
        turned[half] = jnp.transpose(emb_tok[half].reshape(128, 128))
    even = products(64, feats[:, 64:])
    odd = products(65, feats[:, 64:])
    for k, core in others:
        tok_out(k, core).wait_recv()

    for half in range(2):
        rows = [tok[half, :, :, 64 * side : 64 * side + 64].reshape(8, 1, 8, 64) for side in range(2)]
        heads = jnp.concatenate(rows, axis=1).reshape(128, 64)
        turned[half, :64] = jnp.transpose(heads)
    even = even + products(0, feats[:, :64])
    odd = odd + products(1, feats[:, :64])
    result = jnp.concatenate([even, odd], axis=1)
    for d in range(4):
        out_ref[:, d, :] = result[d * 32 : d * 32 + 32]

    for copy_of, args in sent:
        copy_of(*args).wait_send()


def per_device(hidden, input_grad, embedding, vocab_proj, feature_proj, token_ids, targets, doc_ids):
    vmem = pl.BlockSpec(memory_space=pltpu.VMEM)
    bf16, f32, i32 = jnp.bfloat16, jnp.float32, jnp.int32
    dma = pltpu.SemaphoreType.DMA
    na, nb = COUNT[0], COUNT[1]
    out = pl.pallas_call(
        kernel,
        out_shape=jax.ShapeDtypeStruct((32, 4, 128), f32),
        in_specs=[vmem] * 7 + [pl.BlockSpec(memory_space=pl.ANY)],
        out_specs=vmem,
        scratch_shapes=[
            pltpu.VMEM((256, 192), bf16),
            pltpu.VMEM((128, 192), bf16),
            pltpu.VMEM((START[2], D), bf16),
            pltpu.VMEM((4, 4, na, D), bf16),
            pltpu.VMEM((2, 4, 4, nb, D), bf16),
            pltpu.VMEM((2, V_ROWS, D), bf16),
            pltpu.VMEM((2, 128, PAD_ROWS), bf16),
            pltpu.VMEM((4, 4, 8, 128), i32),
            pltpu.VMEM((4, 4 * na, 128), f32),
            pltpu.VMEM((2, 4, 4 * nb, 128), f32),
            pltpu.VMEM((2, 4 * na, 128), f32),
            pltpu.VMEM((2, 2, 4 * nb, 128), f32),
            pltpu.VMEM((4, 4, na, 128), bf16),
            pltpu.VMEM((2, 4, 4, nb, 128), bf16),
            pltpu.VMEM((3, 4, na, 128), bf16),
            pltpu.VMEM((2, 3, 4, nb, 128), bf16),
            pltpu.VMEM((4, na, 128), bf16),
            pltpu.VMEM((2, 4, nb, 128), bf16),
            pltpu.VMEM((3, na, 128), bf16),
            pltpu.VMEM((2, 3, nb, 128), bf16),
            pltpu.VMEM((128, 128), bf16),
            pltpu.VMEM((7, 16, 128), bf16),
            pltpu.VMEM((16, 128), f32),
            pltpu.VMEM((4, na, 128), f32),
            pltpu.VMEM((2, 4, nb, 128), f32),
            pltpu.VMEM((4, na, 128), f32),
            pltpu.VMEM((2, 4, nb, 128), f32),
            pltpu.VMEM((3, na, 128), f32),
            pltpu.VMEM((2, 3, nb, 128), f32),
            pltpu.VMEM((128, 128), f32),
            pltpu.VMEM((7, 16, 128), f32),
            pltpu.VMEM((2, 8, 8, 128), f32),
            pltpu.VMEM((2, 8, 16, 128), f32),
            pltpu.VMEM((2, 8, 16, 128), f32),
            pltpu.VMEM((256, 128), f32),
            pltpu.VMEM((128, 128), f32),
            pltpu.VMEM((128, 128), f32),
            pltpu.VMEM((7, 16, 128), f32),
            pltpu.VMEM((2, 128, 128), f32),
            dma((3,)),
            dma((2, 6)),
            dma((2, 2, 4)),
            dma((2, 2, 3)),
            dma((2, 2, 4, 4)),
            dma((2, 2, 2, 2)),
            dma((2, 2, 2, 2, 4)),
            dma((2, 2, 3)),
            dma((2, 3, 7)),
            dma((2, 2, 3, 3)),
            dma((2, 3, 4)),
            dma((2, 2, 3, 3)),
            dma((2, 2, 7)),
            dma((2, 2, 8)),
        ],
        compiler_params=pltpu.CompilerParams(
            collective_id=0, has_side_effects=True, vmem_limit_bytes=60 * 2**20
        ),
        name="doc_grads",
    )(
        hidden.T, input_grad.T, feature_proj.T, vocab_proj.T,
        targets.reshape(2, 128), token_ids.reshape(2, 128), doc_ids.reshape(2, 128), embedding,
    )
    return out.transpose(1, 0, 2).reshape(4, 4096)


def solution(mesh):
    placed = (
        P("dp", "vocab"),
        P("dp", "vocab"),
        P(("dp", "vocab"), None),
        P(("dp", "vocab"), None),
        P("vocab", None),
        P("dp"),
        P("dp"),
        P("dp"),
    )
    return jax.shard_map(
        per_device, mesh=mesh, in_specs=placed, out_specs=P("dp", None), check_vma=False
    )
```

```python
import jax
import jax.numpy as jnp
from jax import lax
from jax.experimental import pallas as pl
from jax.experimental.pallas import tpu as pltpu
from jax.sharding import PartitionSpec as P

MESH = pl.DeviceIdType.MESH
PRECISE = lax.Precision.HIGHEST
V_ROWS = 501
PAD_ROWS = 512
D = 3072
SLICE = 384
COUNT = (32, 48, 48)
START = (0, 32, 80)
STEP = (1, 3)
HALF = ((((0, 16), (16, 16)),) * 2, (((0, 16), (16, 32)), ((0, 32), (32, 16))))
LAUNCH = 2

SCHEDULE = (
    ((1, 0, 0, 0), (
        ("ZG", 1), ("CX",), ("ZG", 2), ("LK", 0), ("CZ", 0, 0, 1), ("CZ", 1, 0, 1), ("ZG", 3), ("LK", 1),
        ("CY", 2), ("CY", 1), ("CY", 3), ("LK", 2), ("CZ", 0, 0, 2), ("CZ", 1, 0, 2), ("ZG", 4), ("SZ",), ("LK", 3),
        ("LS",), ("CZ", 1, 1, 1), ("S1", 0, 0), ("S1", 0, 1), ("CZ", 0, 1, 1), ("S2", 1, 0, 0), ("S2", 1, 1, 0),
        ("S1", 1, 0), ("S1", 1, 1), ("P2",), ("S2", 0, 0, 0), ("S2", 0, 1, 0), ("CZ", 1, 0, 3), ("CZ", 0, 0, 3),
        ("F1", 0, 0), ("F1", 0, 1), ("CZ", 1, 2, 1), ("CZ", 0, 2, 1), ("F1", 1, 0), ("F1", 1, 1), ("EM",),
    )),
    ((2, 0, 0, 1), (
        ("F2", 1, 0, 0), ("F2", 1, 1, 0), ("CZ", 1, 1, 2), ("CZ", 0, 1, 2), ("CZ", 1, 0, 4), ("S2", 0, 0, 3),
        ("S2", 0, 1, 3), ("CZ", 0, 0, 4),
    )),
    ((2, 1, 1, 0), (
        ("CZ", 1, 2, 2), ("S2", 1, 0, 3), ("S2", 1, 1, 3), ("CZ", 0, 2, 2), ("S2", 0, 0, 1), ("S2", 0, 1, 1),
        ("CZ", 1, 1, 3), ("F2", 0, 0, 0), ("F2", 0, 1, 0), ("CZ", 0, 1, 3), ("CZ", 1, 3, 1), ("S2", 1, 0, 1),
        ("S2", 1, 1, 1), ("CZ", 0, 3, 1), ("S2", 0, 0, 2), ("S2", 0, 1, 2), ("CZ", 1, 2, 3), ("F2", 0, 0, 3),
        ("F2", 0, 1, 3), ("CZ", 0, 2, 3), ("CZ", 1, 1, 4), ("CZ", 0, 1, 4), ("F2", 0, 0, 1),
    )),
    ((1, 1, 1, 1), (
        ("F2", 0, 1, 1), ("S2", 1, 0, 2), ("S2", 1, 1, 2), ("CZ", 1, 3, 2), ("F2", 0, 0, 2), ("F2", 0, 1, 2),
        ("CZ", 0, 3, 2),
    )),
    ((1, 3, 3, 0), (
        ("CZ", 1, 2, 4), ("F2", 1, 0, 3), ("F2", 1, 1, 3), ("CZ", 0, 2, 4), ("FE",),
    )),
    ((2, 3, 3, 1), (
        ("F2", 1, 0, 1), ("F2", 1, 1, 1), ("CZ", 1, 3, 3), ("CZ", 0, 3, 3), ("L1",),
    )),
    ((1, 2, 2, 0), (
        ("F2", 1, 0, 2), ("F2", 1, 1, 2),
    )),
    ((2, 2, 2, 1), (
        ("CZ", 1, 3, 4), ("CZ", 0, 3, 4), ("L2",), ("FW",), ("FIN", 1),
    )),
)


def logits_of(tokens, rows):
    return lax.dot_general(
        tokens, rows, (((1,), (1,)), ((), ())), preferred_element_type=jnp.float32
    )


def mix(parts):
    peaks = [part[:, 65:66] for part in parts]
    top = peaks[0]
    for peak in peaks[1:]:
        top = jnp.maximum(top, peak)
    total = parts[0] * jnp.exp(peaks[0] - top)
    for part, peak in zip(parts[1:], peaks[1:]):
        total = total + part * jnp.exp(peak - top)
    lane = lax.broadcasted_iota(jnp.int32, total.shape, 1)
    return jnp.where(lane == 65, top, total)


def total_of(parts):
    total = parts[0]
    for part in parts[1:]:
        total = total + part
    return total


def pick(step, values):
    chosen = jnp.int32(values[0])
    for number, value in enumerate(values):
        chosen = jnp.where(step == number, jnp.int32(value), chosen)
    return chosen


def kernel(
    hid_in, grad_in, fp_in, vp_in, tgt_in, ids_in, docs_in, emb_ref, out_ref,
    hid_ref, grad_ref, fp_ref, vp_ref, tgt_ref, ids_ref, docs_ref, hidv, rx, gath, hall_a, hall_bc, emb, pet, idb, part_a, part_bc, part_in_a, part_in_bc,
    look_a, look_bc, look_in_a, look_in_bc, look_q_a, look_q_bc, look_q_in_a, look_q_in_bc, look_z, look_z_in, found,
    far_in_a, far_in_bc, q1_a, q1_bc, q1_in_a, q1_in_bc, q2, q2_in, tok, emb_tok, feat, side, sd_in, sz, sz_in, turned,
    sem_in, sem_l, sem_c, sem_zg, sem_cx, sem_cz, sem_1, sem_2, sem_i, sem_s, sem_r, sem_f, sem_q, sem_t, sem_h,
):
    g, v = lax.axis_index("dp"), lax.axis_index("vocab")
    x, y = lax.rem(g, 4), lax.div(g, 4)
    z, c = lax.div(v, 2), lax.rem(v, 2)
    hall = (hall_a, hall_bc.at[0], hall_bc.at[1])
    part = (part_a, part_bc.at[0], part_bc.at[1])
    part_in = (part_in_a, part_in_bc.at[0], part_in_bc.at[1])
    look = (look_a, look_bc.at[0], look_bc.at[1])
    look_in = (look_in_a, look_in_bc.at[0], look_in_bc.at[1])
    q1 = (q1_a, q1_bc.at[0], q1_bc.at[1])
    q1_in = (q1_in_a, q1_in_bc.at[0], q1_in_bc.at[1])
    far_in = (far_in_a, far_in_bc.at[0], far_in_bc.at[1])
    look_q = (look_q_a, look_q_bc.at[0], look_q_bc.at[1])
    look_q_in = (look_q_in_a, look_q_in_bc.at[0], look_q_in_bc.at[1])

    def dev(dx=0, dy=0, dz=0, dc=0):
        return (
            lax.rem(y + dy, 4) * 4 + lax.rem(x + dx, 4),
            lax.rem(z + dz, 8) * 2 + lax.rem(c + dc, 2),
        )

    def remote(src, dst, sems, at, to):
        send, recv = sems.at[(0, *at)], sems.at[(1, *at)]
        return pltpu.make_async_remote_copy(
            src_ref=src, dst_ref=dst, send_sem=send, recv_sem=recv, device_id=to, device_id_type=MESH
        )

    sent = []

    def go(copy_of, *args):
        copy_of(*args).start()
        sent.append((copy_of, args))

    def columns(zz):
        return pl.ds(pl.multiple_of(lax.rem(zz, 8) * SLICE, 128), SLICE)

    row_at, inner_at = (y, x, y), (x, y, x)

    def inner(cls, k):
        return dev(dy=k) if cls == 1 else dev(dx=k)

    def outer(cls, k):
        return dev(dx=k) if cls == 1 else dev(dy=k)

    sources = (hid_in, tgt_in, ids_in, vp_in, fp_in, grad_in, docs_in)
    places = (hid_ref, tgt_ref, ids_ref, vp_ref, fp_ref, grad_ref, docs_ref)
    loads = [pltpu.make_async_copy(src, dst, sem_in.at[n]) for n, (src, dst) in enumerate(zip(sources, places))]
    for load in loads:
        load.start()
    emb_local = pltpu.make_async_copy(emb_ref, emb.at[c], sem_l.at[0])
    emb_local.start()
    barrier = pltpu.get_barrier_semaphore()
    peers = [dev(dc=1)] + [dev(dz=k, dc=core) for k in range(1, 8) for core in (0, 1)]
    peers += [dev(dx=n % 4, dy=n // 4) for n in range(1, 16)]
    for peer in peers:
        pl.semaphore_signal(barrier, inc=1, device_id=peer, device_id_type=MESH)
    for load in loads:
        load.wait()
    first = c == 0
    hidv[...] = jnp.transpose(hid_ref[...].astype(jnp.float32)).astype(jnp.bfloat16)
    row_id = lax.broadcasted_iota(jnp.int32, (8, 128), 0)
    own_tgt = jnp.where(first, tgt_ref[0:1], tgt_ref[1:2])
    own_ids = jnp.where(first, ids_ref[0:1], ids_ref[1:2])
    idb[y, x] = jnp.where(row_id == 0, own_tgt, own_ids)
    pet[c] = jnp.zeros((128, PAD_ROWS), jnp.bfloat16)
    pet[c, :64, :V_ROWS] = vp_ref[...]
    ones_at = lax.broadcasted_iota(jnp.int32, (16, PAD_ROWS), 0) == 0
    in_table = lax.broadcasted_iota(jnp.int32, (16, PAD_ROWS), 1) < V_ROWS
    pet[c, 64:80] = jnp.where(ones_at & in_table, 1.0, 0.0).astype(jnp.bfloat16)
    pl.semaphore_wait(barrier, len(peers))

    other = pl.multiple_of((1 - c) * 128, 128)
    mine = pl.multiple_of(c * 128, 128)

    def hid_swap():
        return remote(hidv.at[pl.ds(other, 128)], rx, sem_c, (0,), dev(dc=1))

    def pet_swap():
        return remote(pet.at[c], pet.at[c], sem_c, (1,), dev(dc=1))

    def emb_swap():
        return remote(emb_ref, emb.at[c], sem_c, (2,), dev(dc=1))

    def side_swap():
        return remote(side.at[pl.ds(other, 128)], sd_in, sem_c, (3,), dev(dc=1))

    def feat_swap():
        return remote(feat.at[c], feat.at[c], sem_c, (4,), dev(dc=1))

    def emb_tok_swap():
        return remote(emb_tok.at[c], emb_tok.at[c], sem_c, (5,), dev(dc=1))

    def ids_out(n):
        return remote(idb.at[y, x], idb.at[y, x], sem_i, (n,), dev(dx=n % 4, dy=n // 4))

    def along_z(way, step):
        at = columns(z + 9 - step) if way == 0 else columns(z + step - 1)
        block = gath.at[:, at]
        return remote(block, block, sem_zg, (way, step - 1), dev(dz=1 if way == 0 else 7))

    def last_x(k):
        block = hall[2].at[y, x, :, columns(z)]
        return remote(block, block, sem_cx, (0, k - 1), dev(dx=k))

    def last_y(k):
        block = hall[2].at[y, :, :, columns(z)]
        return remote(block, block, sem_cx, (1, k - 1), dev(dy=k))

    def last_z(way, sub, step):
        at = columns(z + 9 - step) if way == 0 else columns(z + step - 1)
        row = lax.rem(y + (0, 1, 3, 2)[sub], 4)
        cut = pl.ds(way * 2, 2) if step == 4 else slice(None)
        block = hall[2].at[row, cut, :, at]
        return remote(block, block, sem_cz, (way, sub, step - 1), dev(dz=1 if way == 0 else 7))

    def own_rows(cls):
        return gath.at[pl.ds(START[cls], COUNT[cls])]

    def first_own(cls, way):
        dst = hall[cls].at[row_at[cls], inner_at[cls]]
        return remote(own_rows(cls), dst, sem_1, (cls, way, 0), inner(cls, STEP[way]))

    def first_slice(offset):
        at = columns(z + 8 + offset)
        for cls in (0, 1):
            for way in (0, 1):
                src = gath.at[pl.ds(START[cls], COUNT[cls]), at]
                dst = hall[cls].at[row_at[cls], inner_at[cls], :, at]
                remote(src, dst, sem_1, (cls, way, 0), inner(cls, STEP[way])).start()
                remote(src, dst, sem_2, (cls, way, 0, 0), outer(cls, STEP[way])).start()
                if offset == 0:
                    sent.append((first_own, (cls, way)))
                    sent.append((second_own, (cls, way, 0)))

    def first_on(cls, way):
        pos = lax.rem(inner_at[cls] + 4 - STEP[way], 4)
        block = hall[cls].at[row_at[cls], pos, pl.ds(*HALF[cls][0][way])]
        return remote(block, block, sem_1, (cls, way, 1), inner(cls, STEP[way]))

    def second_own(cls, way, k):
        dst = hall[cls].at[row_at[cls], lax.rem(inner_at[cls] + k, 4)]
        src = own_rows(cls) if k == 0 else dst
        return remote(src, dst, sem_2, (cls, way, 0, k), outer(cls, STEP[way]))

    def second_on(cls, way, k):
        row = lax.rem(row_at[cls] + 4 - STEP[way], 4)
        block = hall[cls].at[row, lax.rem(inner_at[cls] + k, 4), pl.ds(*HALF[cls][k % 2][way])]
        return remote(block, block, sem_2, (cls, way, 1, k), outer(cls, STEP[way]))

    def side_z(k):
        to = pl.multiple_of(lax.rem(z + k, 8) * 16, 16)
        return remote(sz.at[pl.ds(to, 16)], sz_in.at[k - 1], sem_s, (0, k - 1), dev(dz=k))

    def feat_z(k):
        return remote(feat.at[c, z], feat.at[c, z], sem_s, (1, k - 1), dev(dz=k))

    def look_out(cls, k):
        return remote(
            look[cls].at[lax.rem(row_at[cls] + k, 4)], look_in[cls].at[k - 1], sem_r, (0, cls, k - 1), outer(cls, k)
        )

    def look_q_out(cls, k):
        src = look_q[cls].at[lax.rem(inner_at[cls] + k, 4)]
        return remote(src, look_q_in[cls].at[k - 1], sem_q, (1, cls, k - 1), inner(cls, k))

    def look_z_out(k):
        to = pl.multiple_of(lax.rem(z + k, 8) * 16, 16)
        return remote(look_z.at[pl.ds(to, 16)], look_z_in.at[k - 1], sem_s, (2, k - 1), dev(dz=k))

    def part_out(cls, k):
        return remote(part[cls].at[k], part_in[cls].at[k // 2], sem_r, (1, cls, k - 1), outer(cls, k))

    def far_out(cls, j):
        src = part[cls].at[2, pl.ds(pl.multiple_of(lax.rem(inner_at[cls] + j, 4) * COUNT[cls], 16), COUNT[cls])]
        to = dev(dx=2, dy=j) if cls == 1 else dev(dx=j, dy=2)
        return remote(src, far_in[cls].at[j], sem_f, (cls, j), to)

    def q1_out(cls, k):
        src = q1[cls].at[lax.rem(inner_at[cls] + k, 4)]
        return remote(src, q1_in[cls].at[k - 1], sem_q, (0, cls, k - 1), inner(cls, k))

    def q2_out(k):
        to = pl.multiple_of(lax.rem(z + k, 8) * 16, 16)
        return remote(q2.at[pl.ds(to, 16)], q2_in.at[k - 1], sem_t, (0, k - 1), dev(dz=k))

    def emb_tok_out(k):
        return remote(emb_tok.at[c, z], emb_tok.at[c, z], sem_t, (1, k - 1), dev(dz=k))

    def tok_out(k, core):
        return remote(tok.at[c, z], tok.at[c, z], sem_h, (core, k), dev(dz=k, dc=core))

    go(hid_swap)
    go(pet_swap)
    for n in range(1, 16):
        go(ids_out, n)
    hid_swap().wait_recv()
    own_half, got_half = hidv[pl.ds(mine, 128), :], rx[...]
    left = jnp.where(first, own_half, got_half)
    right = jnp.where(first, got_half, own_half)
    both = jnp.concatenate([left, right], axis=1)
    hall_bc[1, y, x, :, columns(z)] = both[START[2] :]
    for k in (1, 3, 2):
        go(last_x, k)
    gath[:, columns(z)] = both[: START[2]]
    for way in (0, 1):
        go(along_z, way, 1)
    first_slice(0)
    go(emb_swap)

    side_t = jnp.concatenate(
        [
            jnp.dot(fp_ref[...], hid_ref[...], preferred_element_type=jnp.float32),
            jnp.dot(fp_ref[...], grad_ref[...], preferred_element_type=jnp.float32),
        ],
        axis=0,
    )
    side[...] = jnp.transpose(side_t)
    go(side_swap)

    keep = [
        pltpu.make_async_copy(own_rows(cls), hall[cls].at[row_at[cls], inner_at[cls]], sem_l.at[1 + cls])
        for cls in (0, 1)
    ]
    row_base = (g * 16 + z * 2) * V_ROWS

    def look_up(gy, gx):
        ids = idb[gy, gx]
        wanted = jnp.concatenate([ids[0:1], ids[1:2]], axis=1) - row_base
        terms = []
        for b in range(2):
            numbers = lax.broadcasted_iota(jnp.int32, (PAD_ROWS, 256), 0) + b * V_ROWS
            hit = jnp.where(numbers == wanted, 1.0, 0.0).astype(jnp.bfloat16)
            terms.append(jnp.dot(pet[b, :64], hit, preferred_element_type=jnp.float32))
        term = total_of(terms)
        stacked = jnp.concatenate([term[:, :128], term[:, 128:]], axis=0)
        rows = jnp.transpose(stacked).astype(jnp.bfloat16)
        look_a[gy, gx] = rows[: START[1]]
        look_bc[0, gx, gy] = rows[START[1] : START[2]]
        look_bc[1, gy, gx] = rows[START[2] :]

    arrived, held = set(), {}

    def handle(what, *at):
        arrived.add((what, *at))
        if what == "CX":
            for k in (1, 2, 3):
                last_x(k).wait_recv()
            for k in (3, 1, 2):
                go(last_y, k)
            for way in (0, 1):
                go(last_z, way, 0, 1)
        elif what == "CY":
            (sub,) = at
            last_y(4 - (0, 1, 3, 2)[sub]).wait_recv()
            if sub == 1:
                for way in (0, 1):
                    go(last_z, way, 1, 1)
        elif what == "CZ":
            way, sub, step = at
            last_z(way, sub, step).wait_recv()
            if step < 4:
                go(last_z, way, sub, step + 1)
            if step == LAUNCH and sub < 2:
                go(last_z, way, sub + 2, 1)
        elif what == "ZG":
            (step,) = at
            for way in (0, 1):
                if step < 4 or way == 0:
                    along_z(way, step).wait_recv()
                if step < 3 or (step == 3 and way == 0):
                    go(along_z, way, step + 1)
            first_slice(-step)
            if step < 4:
                first_slice(step)
            else:
                for copy in keep:
                    copy.start()
        elif what == "S1":
            cls, way = at
            first_own(cls, way).wait_recv()
            go(first_on, cls, way)
        elif what == "P2":
            for k in (3, 1):
                for cls in (0, 1):
                    for way in (0, 1):
                        go(second_own, cls, way, k)
        elif what == "F1":
            cls, way = at
            first_on(cls, way).wait_recv()
            if ("F1", cls, 1 - way) in arrived:
                for to in (0, 1):
                    go(second_own, cls, to, 2)
                for block in held.pop(cls, ()):
                    go(second_on, *block)
        elif what == "S2":
            second_own(*at).wait_recv()
            if True:
                go(second_on, *at)
            else:
                held.setdefault(at[0], []).append(at)
        elif what == "F2":
            second_on(*at).wait_recv()
        elif what == "SZ":
            side_swap().wait_recv()
            sz[...] = side[pl.ds(mine, 128), :] + sd_in[...]
            for k in range(1, 8):
                go(side_z, k)
        elif what == "FE":
            for k in range(1, 8):
                side_z(k).wait_recv()
            own = sz[pl.ds(pl.multiple_of(z * 16, 16), 16), :]
            feat[c, z] = total_of([own] + [sz_in[k] for k in range(7)])
            for k in range(1, 8):
                go(feat_z, k)
        elif what == "FW":
            for k in range(1, 8):
                feat_z(k).wait_recv()
            go(feat_swap)
        elif what == "LK":
            if at[0] == 0:
                pet_swap().wait_recv()
                for n in range(1, 16):
                    ids_out(n).wait_recv()

            def one(gx, carry):
                look_up(at[0], gx)
                return carry

            lax.fori_loop(0, 4, one, 0)
        elif what == "LS":
            for cls in (0, 1, 2):
                for k in (1, 2, 3):
                    go(look_out, cls, k)
        elif what == "EM":
            emb_local.wait()
            emb_swap().wait_recv()
            for copy in keep:
                copy.wait()
        elif what == "L1":
            for cls in (0, 1, 2):
                for k in (1, 2, 3):
                    look_out(cls, k).wait_recv()
                own = look[cls][row_at[cls]]
                look_q[cls][...] = total_of([own] + [look_in[cls][k] for k in range(3)])
                for k in (1, 2, 3):
                    go(look_q_out, cls, k)
        elif what == "L2":
            for cls in (0, 1, 2):
                for k in (1, 2, 3):
                    look_q_out(cls, k).wait_recv()
                own = look_q[cls][inner_at[cls]]
                look_z[START[cls] : START[cls] + COUNT[cls]] = total_of([own] + [look_q_in[cls][k] for k in range(3)])
            for k in range(1, 8):
                go(look_z_out, k)
        elif what == "L3":
            for k in range(1, 8):
                look_z_out(k).wait_recv()
            own = look_z[pl.ds(pl.multiple_of(z * 16, 16), 16), :]
            found[...] = total_of([one.astype(jnp.float32) for one in [own] + [look_z_in[k] for k in range(7)]])
            emb_tok[c, z] = found[...]
            for k in range(1, 8):
                go(emb_tok_out, k)
        elif what == "L4":
            for k in range(1, 8):
                emb_tok_out(k).wait_recv()
            go(emb_tok_swap)
        elif what == "FIN":
            (cls,) = at
            for k in (1, 3):
                part_out(cls, k).wait_recv()
            q1[cls][...] = mix([part[cls][0], part_in[cls][0], part_in[cls][1]]).reshape(4, COUNT[cls], 128)
            for k in (1, 3, 2):
                go(q1_out, cls, k)

    def partial_sums(tokens):
        logits = [logits_of(emb[b], tokens) for b in range(2)]
        top = jnp.maximum(*[jnp.max(one, axis=0, keepdims=True) for one in logits])
        pieces = []
        for b in range(2):
            scaled = jnp.exp(logits[b] - top)
            coarse = scaled.astype(jnp.bfloat16)
            fine = (scaled - coarse.astype(jnp.float32)).astype(jnp.bfloat16)
            table = pet[b, :, :V_ROWS]
            for piece in (coarse, fine):
                pieces.append(jnp.dot(table, piece, preferred_element_type=jnp.float32))
        acc = total_of(pieces)
        row = lax.broadcasted_iota(jnp.int32, acc.shape, 0)
        return jnp.transpose(jnp.where(row == 65, top, acc))

    def tile(step, carry):
        for number, (_, before) in enumerate(SCHEDULE):

            @pl.when(step == number)
            def _(before=before):
                for event in before:
                    handle(*event)

        cls, k, near, half = [pick(step, [which[n] for which, _ in SCHEDULE]) for n in range(4)]
        row = lax.rem(jnp.where(cls == 1, x, y) + k, 4)
        tokens = hall_bc[cls - 1, row].reshape(4 * COUNT[1], D)
        beside = hall_a[lax.rem(y + near, 4), pl.ds(half * 2, 2)].reshape(2 * COUNT[0], D)
        sums = partial_sums(jnp.concatenate([tokens, beside], axis=0))
        part_bc[cls - 1, k] = sums[: 4 * COUNT[1]]
        at = pl.multiple_of(half * 2 * COUNT[0], 2 * COUNT[0])
        part_a[near, pl.ds(at, 2 * COUNT[0])] = sums[4 * COUNT[1] :]

        for number, (which, _) in enumerate(SCHEDULE):

            @pl.when(step == number)
            def _(which=which):
                for one, turn in ((which[0], which[1]), (0, which[2])):
                    if one == 0 and which[3] == 0:
                        continue
                    if turn == 2:
                        for j in (2, 1, 3, 0):
                            go(far_out, one, j)
                    elif turn > 0:
                        go(part_out, one, turn)

        return carry

    lax.fori_loop(0, len(SCHEDULE), tile, 0)

    for cls in (0, 1, 2):
        if ("FIN", cls) not in arrived:
            handle("FIN", cls)
    if ("L3",) not in arrived:
        handle("L3")
    for cls in (0, 1, 2):
        for k in (1, 2, 3):
            q1_out(cls, k).wait_recv()
        for j in range(4):
            far_out(cls, j).wait_recv()
        parts = [q1[cls][inner_at[cls]]] + [q1_in[cls][k] for k in range(3)] + [far_in[cls][j] for j in range(4)]
        q2[START[cls] : START[cls] + COUNT[cls]] = mix(parts)
    for k in (4, 3, 5, 2, 6, 1, 7):
        go(q2_out, k)
    handle("L4")
    for k in range(1, 8):
        q2_out(k).wait_recv()
    mixed = mix([q2[pl.ds(pl.multiple_of(z * 16, 16), 16), :]] + [q2_in[k] for k in range(7)])
    head = mixed[:, :64] / mixed[:, 64:65] - found[:, :64]
    tok[c, z] = jnp.concatenate([head[:8], head[8:]], axis=1)
    others = [(k, core) for k in (4, 3, 5, 2, 6, 1, 7, 0) for core in (0, 1) if (k, core) != (0, 0)]
    for k, core in others:
        go(tok_out, k, core)
    feat_swap().wait_recv()
    emb_tok_swap().wait_recv()
    feats = feat[...].reshape(256, 128)
    local = jnp.concatenate([docs_ref[0:1], docs_ref[1:2]], axis=1) - g * 4
    member = [jnp.where(local == d, 1.0, 0.0) for d in range(4)]

    def products(start, right):
        left = jnp.concatenate([turned[half, pl.ds(start, 32, stride=2), :] for half in range(2)], axis=1)
        left = jnp.concatenate([left * m for m in member], axis=0)
        return jnp.dot(left, right, precision=PRECISE, preferred_element_type=jnp.float32)

    for half in range(2):
        turned[half] = jnp.transpose(emb_tok[half].reshape(128, 128))
    even = products(64, feats[:, 64:])
    odd = products(65, feats[:, 64:])
    for k, core in others:
        tok_out(k, core).wait_recv()

    for half in range(2):
        rows = [tok[half, :, :, 64 * side : 64 * side + 64].reshape(8, 1, 8, 64) for side in range(2)]
        heads = jnp.concatenate(rows, axis=1).reshape(128, 64)
        turned[half, :64] = jnp.transpose(heads)
    even = even + products(0, feats[:, :64])
    odd = odd + products(1, feats[:, :64])
    result = jnp.concatenate([even, odd], axis=1)
    for d in range(4):
        out_ref[:, d, :] = result[d * 32 : d * 32 + 32]

    for copy_of, args in sent:
        copy_of(*args).wait_send()


def per_device(hidden, input_grad, embedding, vocab_proj, feature_proj, token_ids, targets, doc_ids):
    vmem = pl.BlockSpec(memory_space=pltpu.VMEM)
    bf16, f32, i32 = jnp.bfloat16, jnp.float32, jnp.int32
    dma = pltpu.SemaphoreType.DMA
    na, nb = COUNT[0], COUNT[1]
    out = pl.pallas_call(
        kernel,
        out_shape=jax.ShapeDtypeStruct((32, 4, 128), f32),
        in_specs=[pl.BlockSpec(memory_space=pl.ANY)] * 8,
        out_specs=vmem,
        scratch_shapes=[
            pltpu.VMEM((192, 256), bf16),
            pltpu.VMEM((192, 256), bf16),
            pltpu.VMEM((64, 192), bf16),
            pltpu.VMEM((64, V_ROWS), bf16),
            pltpu.VMEM((2, 128), i32),
            pltpu.VMEM((2, 128), i32),
            pltpu.VMEM((2, 128), i32),
            pltpu.VMEM((256, 192), bf16),
            pltpu.VMEM((128, 192), bf16),
            pltpu.VMEM((START[2], D), bf16),
            pltpu.VMEM((4, 4, na, D), bf16),
            pltpu.VMEM((2, 4, 4, nb, D), bf16),
            pltpu.VMEM((2, V_ROWS, D), bf16),
            pltpu.VMEM((2, 128, PAD_ROWS), bf16),
            pltpu.VMEM((4, 4, 8, 128), i32),
            pltpu.VMEM((4, 4 * na, 128), f32),
            pltpu.VMEM((2, 4, 4 * nb, 128), f32),
            pltpu.VMEM((2, 4 * na, 128), f32),
            pltpu.VMEM((2, 2, 4 * nb, 128), f32),
            pltpu.VMEM((4, 4, na, 128), bf16),
            pltpu.VMEM((2, 4, 4, nb, 128), bf16),
            pltpu.VMEM((3, 4, na, 128), bf16),
            pltpu.VMEM((2, 3, 4, nb, 128), bf16),
            pltpu.VMEM((4, na, 128), bf16),
            pltpu.VMEM((2, 4, nb, 128), bf16),
            pltpu.VMEM((3, na, 128), bf16),
            pltpu.VMEM((2, 3, nb, 128), bf16),
            pltpu.VMEM((128, 128), bf16),
            pltpu.VMEM((7, 16, 128), bf16),
            pltpu.VMEM((16, 128), f32),
            pltpu.VMEM((4, na, 128), f32),
            pltpu.VMEM((2, 4, nb, 128), f32),
            pltpu.VMEM((4, na, 128), f32),
            pltpu.VMEM((2, 4, nb, 128), f32),
            pltpu.VMEM((3, na, 128), f32),
            pltpu.VMEM((2, 3, nb, 128), f32),
            pltpu.VMEM((128, 128), f32),
            pltpu.VMEM((7, 16, 128), f32),
            pltpu.VMEM((2, 8, 8, 128), f32),
            pltpu.VMEM((2, 8, 16, 128), f32),
            pltpu.VMEM((2, 8, 16, 128), f32),
            pltpu.VMEM((256, 128), f32),
            pltpu.VMEM((128, 128), f32),
            pltpu.VMEM((128, 128), f32),
            pltpu.VMEM((7, 16, 128), f32),
            pltpu.VMEM((2, 128, 128), f32),
            dma((7,)),
            dma((3,)),
            dma((2, 6)),
            dma((2, 2, 4)),
            dma((2, 2, 3)),
            dma((2, 2, 4, 4)),
            dma((2, 2, 2, 2)),
            dma((2, 2, 2, 2, 4)),
            dma((2, 16)),
            dma((2, 3, 7)),
            dma((2, 2, 3, 3)),
            dma((2, 3, 4)),
            dma((2, 2, 3, 3)),
            dma((2, 2, 7)),
            dma((2, 2, 8)),
        ],
        compiler_params=pltpu.CompilerParams(
            collective_id=0, has_side_effects=True, vmem_limit_bytes=60 * 2**20
        ),
        name="doc_grads",
    )(
        hidden.T, input_grad.T, feature_proj.T, vocab_proj.T,
        targets.reshape(2, 128), token_ids.reshape(2, 128), doc_ids.reshape(2, 128), embedding,
    )
    return out.transpose(1, 0, 2).reshape(4, 4096)


def solution(mesh):
    placed = (
        P("dp", "vocab"),
        P("dp", "vocab"),
        P(("dp", "vocab"), None),
        P(("dp", "vocab"), None),
        P("vocab", None),
        P("dp"),
        P("dp"),
        P("dp"),
    )
    return jax.shard_map(
        per_device, mesh=mesh, in_specs=placed, out_specs=P("dp", None), check_vma=False
    )
```

```python
import jax
import jax.numpy as jnp
from jax import lax
from jax.experimental import pallas as pl
from jax.experimental.pallas import tpu as pltpu
from jax.sharding import PartitionSpec as P

MESH = pl.DeviceIdType.MESH
PRECISE = lax.Precision.HIGHEST
V_ROWS = 501
PAD_ROWS = 512
D = 3072
SLICE = 384
COUNT = (32, 48, 48)
START = (0, 32, 80)
STEP = (1, 3)
HALF = ((((0, 16), (16, 16)),) * 2, (((0, 16), (16, 32)), ((0, 32), (32, 16))))
LAUNCH = 2

SCHEDULE = (
    ((1, 0, 0, 0), (
        ("ZG", 1), ("CX",), ("ZG", 2), ("LK", 0), ("CZ", 0, 0, 1), ("CZ", 1, 0, 1), ("ZG", 3), ("LK", 1),
        ("CY", 2), ("CY", 1), ("CY", 3), ("LK", 2), ("CZ", 0, 0, 2), ("CZ", 1, 0, 2), ("ZG", 4), ("SZ",), ("LK", 3),
        ("LS",), ("CZ", 1, 1, 1), ("S1", 0, 0), ("S1", 0, 1), ("CZ", 0, 1, 1), ("S2", 1, 0, 0), ("S2", 1, 1, 0),
        ("S1", 1, 0), ("S1", 1, 1), ("P2",), ("S2", 0, 0, 0), ("S2", 0, 1, 0), ("CZ", 1, 0, 3), ("CZ", 0, 0, 3),
        ("F1", 0, 0), ("F1", 0, 1), ("CZ", 1, 2, 1), ("CZ", 0, 2, 1), ("F1", 1, 0), ("F1", 1, 1), ("EM",),
    )),
    ((2, 0, 0, 1), (
        ("F2", 1, 0, 0), ("F2", 1, 1, 0), ("CZ", 1, 1, 2), ("CZ", 0, 1, 2), ("CZ", 1, 0, 4), ("S2", 0, 0, 3),
        ("S2", 0, 1, 3), ("CZ", 0, 0, 4),
    )),
    ((2, 1, 1, 0), (
        ("CZ", 1, 2, 2), ("S2", 1, 0, 3), ("S2", 1, 1, 3), ("CZ", 0, 2, 2), ("S2", 0, 0, 1), ("S2", 0, 1, 1),
        ("CZ", 1, 1, 3), ("F2", 0, 0, 0), ("F2", 0, 1, 0), ("CZ", 0, 1, 3), ("CZ", 1, 3, 1), ("S2", 1, 0, 1),
        ("S2", 1, 1, 1), ("CZ", 0, 3, 1), ("S2", 0, 0, 2), ("S2", 0, 1, 2), ("CZ", 1, 2, 3), ("F2", 0, 0, 3),
        ("F2", 0, 1, 3), ("CZ", 0, 2, 3), ("CZ", 1, 1, 4), ("CZ", 0, 1, 4), ("F2", 0, 0, 1), ("L1",),
    )),
    ((1, 1, 1, 1), (
        ("F2", 0, 1, 1), ("S2", 1, 0, 2), ("S2", 1, 1, 2), ("CZ", 1, 3, 2), ("F2", 0, 0, 2), ("F2", 0, 1, 2),
        ("CZ", 0, 3, 2),
    )),
    ((1, 3, 3, 0), (
        ("CZ", 1, 2, 4), ("F2", 1, 0, 3), ("F2", 1, 1, 3), ("CZ", 0, 2, 4), ("FE",),
    )),
    ((2, 3, 3, 1), (
        ("F2", 1, 0, 1), ("F2", 1, 1, 1), ("CZ", 1, 3, 3), ("CZ", 0, 3, 3), ("L2",),
    )),
    ((1, 2, 2, 0), (
        ("F2", 1, 0, 2), ("F2", 1, 1, 2),
    )),
    ((2, 2, 2, 1), (
        ("CZ", 1, 3, 4), ("CZ", 0, 3, 4), ("FW",), ("L3",), ("FIN", 1),
    )),
)


def logits_of(tokens, rows):
    return lax.dot_general(
        tokens, rows, (((1,), (1,)), ((), ())), preferred_element_type=jnp.float32
    )


def mix(parts):
    peaks = [part[:, 65:66] for part in parts]
    top = peaks[0]
    for peak in peaks[1:]:
        top = jnp.maximum(top, peak)
    total = parts[0] * jnp.exp(peaks[0] - top)
    for part, peak in zip(parts[1:], peaks[1:]):
        total = total + part * jnp.exp(peak - top)
    lane = lax.broadcasted_iota(jnp.int32, total.shape, 1)
    return jnp.where(lane == 65, top, total)


def total_of(parts):
    total = parts[0]
    for part in parts[1:]:
        total = total + part
    return total


def pick(step, values):
    chosen = jnp.int32(values[0])
    for number, value in enumerate(values):
        chosen = jnp.where(step == number, jnp.int32(value), chosen)
    return chosen


def kernel(
    hid_in, grad_in, fp_in, vp_in, tgt_in, ids_in, docs_in, emb_ref, out_ref,
    hid_ref, grad_ref, fp_ref, vp_ref, tgt_ref, ids_ref, docs_ref, hidv, rx, gath, hall_a, hall_bc, emb, pet, idb, part_a, part_bc, part_in_a, part_in_bc,
    look_a, look_bc, look_in_a, look_in_bc, look_q_a, look_q_bc, look_q_in_a, look_q_in_bc, look_z, look_z_in, found,
    far_in_a, far_in_bc, q1_a, q1_bc, q1_in_a, q1_in_bc, q2, q2_in, tok, emb_tok, feat, side, sd_in, sz, sz_in, turned,
    sem_in, sem_l, sem_c, sem_zg, sem_cx, sem_cz, sem_1, sem_2, sem_i, sem_s, sem_r, sem_f, sem_q, sem_t, sem_h,
):
    g, v = lax.axis_index("dp"), lax.axis_index("vocab")
    x, y = lax.rem(g, 4), lax.div(g, 4)
    z, c = lax.div(v, 2), lax.rem(v, 2)
    hall = (hall_a, hall_bc.at[0], hall_bc.at[1])
    part = (part_a, part_bc.at[0], part_bc.at[1])
    part_in = (part_in_a, part_in_bc.at[0], part_in_bc.at[1])
    look = (look_a, look_bc.at[0], look_bc.at[1])
    look_in = (look_in_a, look_in_bc.at[0], look_in_bc.at[1])
    q1 = (q1_a, q1_bc.at[0], q1_bc.at[1])
    q1_in = (q1_in_a, q1_in_bc.at[0], q1_in_bc.at[1])
    far_in = (far_in_a, far_in_bc.at[0], far_in_bc.at[1])
    look_q = (look_q_a, look_q_bc.at[0], look_q_bc.at[1])
    look_q_in = (look_q_in_a, look_q_in_bc.at[0], look_q_in_bc.at[1])

    def dev(dx=0, dy=0, dz=0, dc=0):
        return (
            lax.rem(y + dy, 4) * 4 + lax.rem(x + dx, 4),
            lax.rem(z + dz, 8) * 2 + lax.rem(c + dc, 2),
        )

    def remote(src, dst, sems, at, to):
        send, recv = sems.at[(0, *at)], sems.at[(1, *at)]
        return pltpu.make_async_remote_copy(
            src_ref=src, dst_ref=dst, send_sem=send, recv_sem=recv, device_id=to, device_id_type=MESH
        )

    sent = []

    def go(copy_of, *args):
        copy_of(*args).start()
        sent.append((copy_of, args))

    def columns(zz):
        return pl.ds(pl.multiple_of(lax.rem(zz, 8) * SLICE, 128), SLICE)

    row_at, inner_at = (y, x, y), (x, y, x)

    def inner(cls, k):
        return dev(dy=k) if cls == 1 else dev(dx=k)

    def outer(cls, k):
        return dev(dx=k) if cls == 1 else dev(dy=k)

    sources = (hid_in, tgt_in, ids_in, vp_in, fp_in, grad_in, docs_in)
    places = (hid_ref, tgt_ref, ids_ref, vp_ref, fp_ref, grad_ref, docs_ref)
    loads = [pltpu.make_async_copy(src, dst, sem_in.at[n]) for n, (src, dst) in enumerate(zip(sources, places))]
    for load in loads:
        load.start()
    emb_local = pltpu.make_async_copy(emb_ref, emb.at[c], sem_l.at[0])
    emb_local.start()
    barrier = pltpu.get_barrier_semaphore()
    peers = [dev(dc=1)] + [dev(dz=k, dc=core) for k in range(1, 8) for core in (0, 1)]
    peers += [dev(dx=n % 4, dy=n // 4) for n in range(1, 16)]
    for peer in peers:
        pl.semaphore_signal(barrier, inc=1, device_id=peer, device_id_type=MESH)
    for load in loads:
        load.wait()
    first = c == 0
    hidv[...] = jnp.transpose(hid_ref[...].astype(jnp.float32)).astype(jnp.bfloat16)
    row_id = lax.broadcasted_iota(jnp.int32, (8, 128), 0)
    own_tgt = jnp.where(first, tgt_ref[0:1], tgt_ref[1:2])
    own_ids = jnp.where(first, ids_ref[0:1], ids_ref[1:2])
    idb[y, x] = jnp.where(row_id == 0, own_tgt, own_ids)
    pet[c] = jnp.zeros((128, PAD_ROWS), jnp.bfloat16)
    pet[c, :64, :V_ROWS] = vp_ref[...]
    ones_at = lax.broadcasted_iota(jnp.int32, (16, PAD_ROWS), 0) == 0
    in_table = lax.broadcasted_iota(jnp.int32, (16, PAD_ROWS), 1) < V_ROWS
    pet[c, 64:80] = jnp.where(ones_at & in_table, 1.0, 0.0).astype(jnp.bfloat16)
    pl.semaphore_wait(barrier, len(peers))

    other = pl.multiple_of((1 - c) * 128, 128)
    mine = pl.multiple_of(c * 128, 128)

    def hid_swap():
        return remote(hidv.at[pl.ds(other, 128)], rx, sem_c, (0,), dev(dc=1))

    def pet_swap():
        return remote(pet.at[c], pet.at[c], sem_c, (1,), dev(dc=1))

    def emb_swap():
        return remote(emb_ref, emb.at[c], sem_c, (2,), dev(dc=1))

    def side_swap():
        return remote(side.at[pl.ds(other, 128)], sd_in, sem_c, (3,), dev(dc=1))

    def feat_swap():
        return remote(feat.at[c], feat.at[c], sem_c, (4,), dev(dc=1))

    def emb_tok_swap():
        return remote(emb_tok.at[c], emb_tok.at[c], sem_c, (5,), dev(dc=1))

    def ids_out(n):
        return remote(idb.at[y, x], idb.at[y, x], sem_i, (n,), dev(dx=n % 4, dy=n // 4))

    def along_z(way, step):
        at = columns(z + 9 - step) if way == 0 else columns(z + step - 1)
        block = gath.at[:, at]
        return remote(block, block, sem_zg, (way, step - 1), dev(dz=1 if way == 0 else 7))

    def last_x(k):
        block = hall[2].at[y, x, :, columns(z)]
        return remote(block, block, sem_cx, (0, k - 1), dev(dx=k))

    def last_y(k):
        block = hall[2].at[y, :, :, columns(z)]
        return remote(block, block, sem_cx, (1, k - 1), dev(dy=k))

    def last_z(way, sub, step):
        at = columns(z + 9 - step) if way == 0 else columns(z + step - 1)
        row = lax.rem(y + (0, 1, 3, 2)[sub], 4)
        cut = pl.ds(way * 2, 2) if step == 4 else slice(None)
        block = hall[2].at[row, cut, :, at]
        return remote(block, block, sem_cz, (way, sub, step - 1), dev(dz=1 if way == 0 else 7))

    def own_rows(cls):
        return gath.at[pl.ds(START[cls], COUNT[cls])]

    def first_own(cls, way):
        dst = hall[cls].at[row_at[cls], inner_at[cls]]
        return remote(own_rows(cls), dst, sem_1, (cls, way, 0), inner(cls, STEP[way]))

    def first_slice(offset):
        at = columns(z + 8 + offset)
        for cls in (0, 1):
            for way in (0, 1):
                src = gath.at[pl.ds(START[cls], COUNT[cls]), at]
                dst = hall[cls].at[row_at[cls], inner_at[cls], :, at]
                remote(src, dst, sem_1, (cls, way, 0), inner(cls, STEP[way])).start()
                remote(src, dst, sem_2, (cls, way, 0, 0), outer(cls, STEP[way])).start()
                if offset == 0:
                    sent.append((first_own, (cls, way)))
                    sent.append((second_own, (cls, way, 0)))

    def first_on(cls, way):
        pos = lax.rem(inner_at[cls] + 4 - STEP[way], 4)
        block = hall[cls].at[row_at[cls], pos, pl.ds(*HALF[cls][0][way])]
        return remote(block, block, sem_1, (cls, way, 1), inner(cls, STEP[way]))

    def second_own(cls, way, k):
        dst = hall[cls].at[row_at[cls], lax.rem(inner_at[cls] + k, 4)]
        src = own_rows(cls) if k == 0 else dst
        return remote(src, dst, sem_2, (cls, way, 0, k), outer(cls, STEP[way]))

    def second_on(cls, way, k):
        row = lax.rem(row_at[cls] + 4 - STEP[way], 4)
        block = hall[cls].at[row, lax.rem(inner_at[cls] + k, 4), pl.ds(*HALF[cls][k % 2][way])]
        return remote(block, block, sem_2, (cls, way, 1, k), outer(cls, STEP[way]))

    def side_z(k):
        to = pl.multiple_of(lax.rem(z + k, 8) * 16, 16)
        return remote(sz.at[pl.ds(to, 16)], sz_in.at[k - 1], sem_s, (0, k - 1), dev(dz=k))

    def feat_z(k):
        return remote(feat.at[c, z], feat.at[c, z], sem_s, (1, k - 1), dev(dz=k))

    def look_out(cls, k):
        return remote(
            look[cls].at[lax.rem(row_at[cls] + k, 4)], look_in[cls].at[k - 1], sem_r, (0, cls, k - 1), outer(cls, k)
        )

    def look_q_out(cls, k):
        src = look_q[cls].at[lax.rem(inner_at[cls] + k, 4)]
        return remote(src, look_q_in[cls].at[k - 1], sem_q, (1, cls, k - 1), inner(cls, k))

    def look_z_out(k):
        to = pl.multiple_of(lax.rem(z + k, 8) * 16, 16)
        return remote(look_z.at[pl.ds(to, 16)], look_z_in.at[k - 1], sem_s, (2, k - 1), dev(dz=k))

    def part_out(cls, k):
        return remote(part[cls].at[k], part_in[cls].at[k // 2], sem_r, (1, cls, k - 1), outer(cls, k))

    def far_out(cls, j):
        src = part[cls].at[2, pl.ds(pl.multiple_of(lax.rem(inner_at[cls] + j, 4) * COUNT[cls], 16), COUNT[cls])]
        to = dev(dx=2, dy=j) if cls == 1 else dev(dx=j, dy=2)
        return remote(src, far_in[cls].at[j], sem_f, (cls, j), to)

    def q1_out(cls, k):
        src = q1[cls].at[lax.rem(inner_at[cls] + k, 4)]
        return remote(src, q1_in[cls].at[k - 1], sem_q, (0, cls, k - 1), inner(cls, k))

    def q2_out(k):
        to = pl.multiple_of(lax.rem(z + k, 8) * 16, 16)
        return remote(q2.at[pl.ds(to, 16)], q2_in.at[k - 1], sem_t, (0, k - 1), dev(dz=k))

    def emb_tok_out(k):
        return remote(emb_tok.at[c, z], emb_tok.at[c, z], sem_t, (1, k - 1), dev(dz=k))

    def tok_out(k, core):
        return remote(tok.at[c, z], tok.at[c, z], sem_h, (core, k), dev(dz=k, dc=core))

    go(hid_swap)
    go(pet_swap)
    for n in range(1, 16):
        go(ids_out, n)
    hid_swap().wait_recv()
    own_half, got_half = hidv[pl.ds(mine, 128), :], rx[...]
    left = jnp.where(first, own_half, got_half)
    right = jnp.where(first, got_half, own_half)
    both = jnp.concatenate([left, right], axis=1)
    hall_bc[1, y, x, :, columns(z)] = both[START[2] :]
    for k in (1, 3, 2):
        go(last_x, k)
    gath[:, columns(z)] = both[: START[2]]
    for way in (0, 1):
        go(along_z, way, 1)
    first_slice(0)
    go(emb_swap)

    side_t = jnp.concatenate(
        [
            jnp.dot(fp_ref[...], hid_ref[...], preferred_element_type=jnp.float32),
            jnp.dot(fp_ref[...], grad_ref[...], preferred_element_type=jnp.float32),
        ],
        axis=0,
    )
    side[...] = jnp.transpose(side_t)
    go(side_swap)

    keep = [
        pltpu.make_async_copy(own_rows(cls), hall[cls].at[row_at[cls], inner_at[cls]], sem_l.at[1 + cls])
        for cls in (0, 1)
    ]
    row_base = (g * 16 + z * 2) * V_ROWS

    def look_up(gy, gx):
        ids = idb[gy, gx]
        wanted = jnp.concatenate([ids[0:1], ids[1:2]], axis=1) - row_base
        terms = []
        for b in range(2):
            numbers = lax.broadcasted_iota(jnp.int32, (PAD_ROWS, 256), 0) + b * V_ROWS
            hit = jnp.where(numbers == wanted, 1.0, 0.0).astype(jnp.bfloat16)
            terms.append(jnp.dot(pet[b, :64], hit, preferred_element_type=jnp.float32))
        term = total_of(terms)
        stacked = jnp.concatenate([term[:, :128], term[:, 128:]], axis=0)
        rows = jnp.transpose(stacked).astype(jnp.bfloat16)
        look_a[gy, gx] = rows[: START[1]]
        look_bc[0, gx, gy] = rows[START[1] : START[2]]
        look_bc[1, gy, gx] = rows[START[2] :]

    arrived, held = set(), {}

    def handle(what, *at):
        arrived.add((what, *at))
        if what == "CX":
            for k in (1, 2, 3):
                last_x(k).wait_recv()
            for k in (3, 1, 2):
                go(last_y, k)
            for way in (0, 1):
                go(last_z, way, 0, 1)
        elif what == "CY":
            (sub,) = at
            last_y(4 - (0, 1, 3, 2)[sub]).wait_recv()
            if sub == 1:
                for way in (0, 1):
                    go(last_z, way, 1, 1)
        elif what == "CZ":
            way, sub, step = at
            last_z(way, sub, step).wait_recv()
            if step < 4:
                go(last_z, way, sub, step + 1)
            if step == LAUNCH and sub < 2:
                go(last_z, way, sub + 2, 1)
        elif what == "ZG":
            (step,) = at
            for way in (0, 1):
                if step < 4 or way == 0:
                    along_z(way, step).wait_recv()
                if step < 3 or (step == 3 and way == 0):
                    go(along_z, way, step + 1)
            first_slice(-step)
            if step < 4:
                first_slice(step)
            else:
                for copy in keep:
                    copy.start()
        elif what == "S1":
            cls, way = at
            first_own(cls, way).wait_recv()
            go(first_on, cls, way)
        elif what == "P2":
            for k in (3, 1):
                for cls in (0, 1):
                    for way in (0, 1):
                        go(second_own, cls, way, k)
        elif what == "F1":
            cls, way = at
            first_on(cls, way).wait_recv()
            if ("F1", cls, 1 - way) in arrived:
                for to in (0, 1):
                    go(second_own, cls, to, 2)
                for block in held.pop(cls, ()):
                    go(second_on, *block)
        elif what == "S2":
            second_own(*at).wait_recv()
            if True:
                go(second_on, *at)
            else:
                held.setdefault(at[0], []).append(at)
        elif what == "F2":
            second_on(*at).wait_recv()
        elif what == "SZ":
            side_swap().wait_recv()
            sz[...] = side[pl.ds(mine, 128), :] + sd_in[...]
            for k in range(1, 8):
                go(side_z, k)
        elif what == "FE":
            for k in range(1, 8):
                side_z(k).wait_recv()
            own = sz[pl.ds(pl.multiple_of(z * 16, 16), 16), :]
            feat[c, z] = total_of([own] + [sz_in[k] for k in range(7)])
            for k in range(1, 8):
                go(feat_z, k)
        elif what == "FW":
            for k in range(1, 8):
                feat_z(k).wait_recv()
            go(feat_swap)
        elif what == "LK":
            if at[0] == 0:
                pet_swap().wait_recv()
                for n in range(1, 16):
                    ids_out(n).wait_recv()

            def one(gx, carry):
                look_up(at[0], gx)
                return carry

            lax.fori_loop(0, 4, one, 0)
        elif what == "LS":
            for cls in (0, 1, 2):
                for k in (1, 2, 3):
                    go(look_out, cls, k)
        elif what == "EM":
            emb_local.wait()
            emb_swap().wait_recv()
            for copy in keep:
                copy.wait()
        elif what == "L1":
            for cls in (0, 1, 2):
                for k in (1, 2, 3):
                    look_out(cls, k).wait_recv()
                own = look[cls][row_at[cls]]
                look_q[cls][...] = total_of([own] + [look_in[cls][k] for k in range(3)])
                for k in (1, 2, 3):
                    go(look_q_out, cls, k)
        elif what == "L2":
            for cls in (0, 1, 2):
                for k in (1, 2, 3):
                    look_q_out(cls, k).wait_recv()
                own = look_q[cls][inner_at[cls]]
                look_z[START[cls] : START[cls] + COUNT[cls]] = total_of([own] + [look_q_in[cls][k] for k in range(3)])
            for k in range(1, 8):
                go(look_z_out, k)
        elif what == "L3":
            for k in range(1, 8):
                look_z_out(k).wait_recv()
            own = look_z[pl.ds(pl.multiple_of(z * 16, 16), 16), :]
            found[...] = total_of([one.astype(jnp.float32) for one in [own] + [look_z_in[k] for k in range(7)]])
            emb_tok[c, z] = found[...]
            for k in range(1, 8):
                go(emb_tok_out, k)
        elif what == "L4":
            for k in range(1, 8):
                emb_tok_out(k).wait_recv()
            go(emb_tok_swap)
        elif what == "FIN":
            (cls,) = at
            for k in (1, 3):
                part_out(cls, k).wait_recv()
            q1[cls][...] = mix([part[cls][0], part_in[cls][0], part_in[cls][1]]).reshape(4, COUNT[cls], 128)
            for k in (1, 3, 2):
                go(q1_out, cls, k)

    def partial_sums(tokens):
        logits = [logits_of(emb[b], tokens) for b in range(2)]
        top = jnp.maximum(*[jnp.max(one, axis=0, keepdims=True) for one in logits])
        pieces = []
        for b in range(2):
            scaled = jnp.exp(logits[b] - top)
            coarse = scaled.astype(jnp.bfloat16)
            fine = (scaled - coarse.astype(jnp.float32)).astype(jnp.bfloat16)
            table = pet[b, :, :V_ROWS]
            for piece in (coarse, fine):
                pieces.append(jnp.dot(table, piece, preferred_element_type=jnp.float32))
        acc = total_of(pieces)
        row = lax.broadcasted_iota(jnp.int32, acc.shape, 0)
        return jnp.transpose(jnp.where(row == 65, top, acc))

    def tile(step, carry):
        for number, (_, before) in enumerate(SCHEDULE):

            @pl.when(step == number)
            def _(before=before):
                for event in before:
                    handle(*event)

        cls, k, near, half = [pick(step, [which[n] for which, _ in SCHEDULE]) for n in range(4)]
        row = lax.rem(jnp.where(cls == 1, x, y) + k, 4)
        tokens = hall_bc[cls - 1, row].reshape(4 * COUNT[1], D)
        beside = hall_a[lax.rem(y + near, 4), pl.ds(half * 2, 2)].reshape(2 * COUNT[0], D)
        sums = partial_sums(jnp.concatenate([tokens, beside], axis=0))
        part_bc[cls - 1, k] = sums[: 4 * COUNT[1]]
        at = pl.multiple_of(half * 2 * COUNT[0], 2 * COUNT[0])
        part_a[near, pl.ds(at, 2 * COUNT[0])] = sums[4 * COUNT[1] :]

        for number, (which, _) in enumerate(SCHEDULE):

            @pl.when(step == number)
            def _(which=which):
                for one, turn in ((which[0], which[1]), (0, which[2])):
                    if one == 0 and which[3] == 0:
                        continue
                    if turn == 2:
                        for j in (2, 1, 3, 0):
                            go(far_out, one, j)
                    elif turn > 0:
                        go(part_out, one, turn)

        return carry

    lax.fori_loop(0, len(SCHEDULE), tile, 0)

    for cls in (0, 1, 2):
        if ("FIN", cls) not in arrived:
            handle("FIN", cls)
    if ("L3",) not in arrived:
        handle("L3")
    for cls in (0, 1, 2):
        for k in (1, 2, 3):
            q1_out(cls, k).wait_recv()
        for j in range(4):
            far_out(cls, j).wait_recv()
        parts = [q1[cls][inner_at[cls]]] + [q1_in[cls][k] for k in range(3)] + [far_in[cls][j] for j in range(4)]
        q2[START[cls] : START[cls] + COUNT[cls]] = mix(parts)
    for k in (4, 3, 5, 2, 6, 1, 7):
        go(q2_out, k)
    handle("L4")
    for k in range(1, 8):
        q2_out(k).wait_recv()
    mixed = mix([q2[pl.ds(pl.multiple_of(z * 16, 16), 16), :]] + [q2_in[k] for k in range(7)])
    head = mixed[:, :64] / mixed[:, 64:65] - found[:, :64]
    tok[c, z] = jnp.concatenate([head[:8], head[8:]], axis=1)
    others = [(k, core) for k in (4, 3, 5, 2, 6, 1, 7, 0) for core in (0, 1) if (k, core) != (0, 0)]
    for k, core in others:
        go(tok_out, k, core)
    feat_swap().wait_recv()
    emb_tok_swap().wait_recv()
    feats = feat[...].reshape(256, 128)
    local = jnp.concatenate([docs_ref[0:1], docs_ref[1:2]], axis=1) - g * 4
    member = [jnp.where(local == d, 1.0, 0.0) for d in range(4)]

    def products(start, right):
        left = jnp.concatenate([turned[half, pl.ds(start, 32, stride=2), :] for half in range(2)], axis=1)
        left = jnp.concatenate([left * m for m in member], axis=0)
        return jnp.dot(left, right, precision=PRECISE, preferred_element_type=jnp.float32)

    for half in range(2):
        turned[half] = jnp.transpose(emb_tok[half].reshape(128, 128))
    even = products(64, feats[:, 64:])
    odd = products(65, feats[:, 64:])
    for k, core in others:
        tok_out(k, core).wait_recv()

    for half in range(2):
        rows = [tok[half, :, :, 64 * side : 64 * side + 64].reshape(8, 1, 8, 64) for side in range(2)]
        heads = jnp.concatenate(rows, axis=1).reshape(128, 64)
        turned[half, :64] = jnp.transpose(heads)
    even = even + products(0, feats[:, :64])
    odd = odd + products(1, feats[:, :64])
    result = jnp.concatenate([even, odd], axis=1)
    for d in range(4):
        out_ref[:, d, :] = result[d * 32 : d * 32 + 32]

    for copy_of, args in sent:
        copy_of(*args).wait_send()


def per_device(hidden, input_grad, embedding, vocab_proj, feature_proj, token_ids, targets, doc_ids):
    vmem = pl.BlockSpec(memory_space=pltpu.VMEM)
    bf16, f32, i32 = jnp.bfloat16, jnp.float32, jnp.int32
    dma = pltpu.SemaphoreType.DMA
    na, nb = COUNT[0], COUNT[1]
    out = pl.pallas_call(
        kernel,
        out_shape=jax.ShapeDtypeStruct((32, 4, 128), f32),
        in_specs=[pl.BlockSpec(memory_space=pl.ANY)] * 8,
        out_specs=vmem,
        scratch_shapes=[
            pltpu.VMEM((192, 256), bf16),
            pltpu.VMEM((192, 256), bf16),
            pltpu.VMEM((64, 192), bf16),
            pltpu.VMEM((64, V_ROWS), bf16),
            pltpu.VMEM((2, 128), i32),
            pltpu.VMEM((2, 128), i32),
            pltpu.VMEM((2, 128), i32),
            pltpu.VMEM((256, 192), bf16),
            pltpu.VMEM((128, 192), bf16),
            pltpu.VMEM((START[2], D), bf16),
            pltpu.VMEM((4, 4, na, D), bf16),
            pltpu.VMEM((2, 4, 4, nb, D), bf16),
            pltpu.VMEM((2, V_ROWS, D), bf16),
            pltpu.VMEM((2, 128, PAD_ROWS), bf16),
            pltpu.VMEM((4, 4, 8, 128), i32),
            pltpu.VMEM((4, 4 * na, 128), f32),
            pltpu.VMEM((2, 4, 4 * nb, 128), f32),
            pltpu.VMEM((2, 4 * na, 128), f32),
            pltpu.VMEM((2, 2, 4 * nb, 128), f32),
            pltpu.VMEM((4, 4, na, 128), bf16),
            pltpu.VMEM((2, 4, 4, nb, 128), bf16),
            pltpu.VMEM((3, 4, na, 128), bf16),
            pltpu.VMEM((2, 3, 4, nb, 128), bf16),
            pltpu.VMEM((4, na, 128), bf16),
            pltpu.VMEM((2, 4, nb, 128), bf16),
            pltpu.VMEM((3, na, 128), bf16),
            pltpu.VMEM((2, 3, nb, 128), bf16),
            pltpu.VMEM((128, 128), bf16),
            pltpu.VMEM((7, 16, 128), bf16),
            pltpu.VMEM((16, 128), f32),
            pltpu.VMEM((4, na, 128), f32),
            pltpu.VMEM((2, 4, nb, 128), f32),
            pltpu.VMEM((4, na, 128), f32),
            pltpu.VMEM((2, 4, nb, 128), f32),
            pltpu.VMEM((3, na, 128), f32),
            pltpu.VMEM((2, 3, nb, 128), f32),
            pltpu.VMEM((128, 128), f32),
            pltpu.VMEM((7, 16, 128), f32),
            pltpu.VMEM((2, 8, 8, 128), f32),
            pltpu.VMEM((2, 8, 16, 128), f32),
            pltpu.VMEM((2, 8, 16, 128), f32),
            pltpu.VMEM((256, 128), f32),
            pltpu.VMEM((128, 128), f32),
            pltpu.VMEM((128, 128), f32),
            pltpu.VMEM((7, 16, 128), f32),
            pltpu.VMEM((2, 128, 128), f32),
            dma((7,)),
            dma((3,)),
            dma((2, 6)),
            dma((2, 2, 4)),
            dma((2, 2, 3)),
            dma((2, 2, 4, 4)),
            dma((2, 2, 2, 2)),
            dma((2, 2, 2, 2, 4)),
            dma((2, 16)),
            dma((2, 3, 7)),
            dma((2, 2, 3, 3)),
            dma((2, 3, 4)),
            dma((2, 2, 3, 3)),
            dma((2, 2, 7)),
            dma((2, 2, 8)),
        ],
        compiler_params=pltpu.CompilerParams(
            collective_id=0, has_side_effects=True, vmem_limit_bytes=60 * 2**20
        ),
        name="doc_grads",
    )(
        hidden.T, input_grad.T, feature_proj.T, vocab_proj.T,
        targets.reshape(2, 128), token_ids.reshape(2, 128), doc_ids.reshape(2, 128), embedding,
    )
    return out.transpose(1, 0, 2).reshape(4, 4096)


def solution(mesh):
    placed = (
        P("dp", "vocab"),
        P("dp", "vocab"),
        P(("dp", "vocab"), None),
        P(("dp", "vocab"), None),
        P("vocab", None),
        P("dp"),
        P("dp"),
        P("dp"),
    )
    return jax.shard_map(
        per_device, mesh=mesh, in_specs=placed, out_specs=P("dp", None), check_vma=False
    )
```
